256 devices in a mesh: leaf: 256 (over z, x, y, core).
Axes of the slice: x: 4, y: 4, z: 8, core: 2. Of those that a mesh axis runs over, the one named last changes fastest.
Arguments:
- sources: float32 [2, 4096, 8, 256], P(None, 'leaf'), may hold values from -6 to 6
- leaf_slot: int32 [4096], replicated, may hold values from 0 to 4095, as said below
- in_basis: float32 [4096, 2, 64, 256], P('leaf'), may hold values from -0.25 to 0.25
- butterfly: float32 [8, 256, 2, 64, 128], P(None, 'leaf'), may hold values from -0.375 to 0.375
- out_basis: float32 [4096, 2, 64, 256], P('leaf'), may hold values from -0.5 to 0.5
- near_pairs: int32 [2048, 2], P('leaf'), may hold values from 0 to 4095, as said below
- near_count: int32 [256], P('leaf'), may hold values from 1 to 8, as said below
- near_blocks: float32 [2048, 2, 256, 256], P('leaf'), may hold values from -0.25 to 0.25
Outputs:
- field: float32 [2, 4096, 8, 256], P(None, 'leaf')
The draws below stay inside these ranges and needn't reach their ends.
Inputs may be any that keep to these rules, and one draw needn't show every extreme that they name: Leaf l is stored on its own device: leaf_slot restricted to leaves d * 16 .. (d + 1) * 16 - 1 is a permutation of those same slots. `near_pairs`: column 0 is the source leaf, column 1 the target leaf. The target leaf of a slot of device d is one of d's leaves d * 16 .. (d + 1) * 16 - 1, and source and target leaves lie at most 4 apart along the line. `near_count`: some device has all 8 slots live.
All inputs are finite; a program needn't handle non-finite values.
Results may differ from the reference program's by a relative error of at most 0.00011.
Values sent between devices are 32-bit elements; how exact they have to be, the bound alone decides.
A program may use at most 64 MiB of HBM per device.

```python
import jax
import jax.numpy as jnp
from jax import lax

P_SIZE = 256
R = 64
S = 8
LEAF_DEV = 16
NEAR_DEV = 8
EDGE = 4
LEAVES = 4096
NEAR_TOTAL = 2048
LEVELS = 8
N_LEAF = 256


def draw_leaf_slot(key, part):
    key = jax.random.fold_in(key, 1)
    scores = jax.random.randint(key, (N_LEAF, LEAF_DEV), 0, 1 << 20) * LEAF_DEV + jnp.arange(LEAF_DEV, dtype=jnp.int32)[None, :]
    order = jnp.argsort(scores, axis=1, stable=True).astype(jnp.int32)
    slots = order + (jnp.arange(N_LEAF, dtype=jnp.int32) * LEAF_DEV)[:, None]
    return slots.reshape(-1).astype(jnp.int32)


def draw_near_pairs(key, part):
    key = jax.random.fold_in(key, 2)
    key_one, key_two, key_three = jax.random.split(key, 3)
    index_all = jnp.arange(NEAR_TOTAL, dtype=jnp.int32)
    device = index_all // NEAR_DEV
    within = index_all % NEAR_DEV
    base = device * LEAF_DEV
    any_target = base + jax.random.randint(key_one, (NEAR_TOTAL,), 0, LEAF_DEV)
    any_source = jnp.clip(any_target + jax.random.randint(key_two, (NEAR_TOTAL,), -EDGE, EDGE + 1), 0, LEAVES - 1)
    offset = jax.random.randint(key_three, (NEAR_TOTAL,), 0, EDGE)
    low_target = base
    low_source = jnp.where(device > 0, base - 1 - offset, base + 1 + offset)
    high_target = base + LEAF_DEV - 1
    high_source = jnp.where(device < N_LEAF - 1, base + LEAF_DEV + offset, base + LEAF_DEV - 2 - offset)
    target = jnp.where(within == 0, low_target, jnp.where(within == 1, high_target, any_target))
    source = jnp.where(within == 0, low_source, jnp.where(within == 1, high_source, any_source))
    return jnp.stack([source, target], axis=1).astype(jnp.int32)


def draw_near_count(key, part):
    key = jax.random.fold_in(key, 3)
    key_one, key_two = jax.random.split(key)
    counts = jax.random.randint(key_one, (N_LEAF,), 1, NEAR_DEV + 1)
    fullest = jax.random.randint(key_two, (), 0, N_LEAF)
    return jnp.where(jnp.arange(N_LEAF, dtype=jnp.int32) == fullest, NEAR_DEV, counts).astype(jnp.int32)


def steps_of(own_key, shape, shards, smallest, high):
    level = 1.0
    for position, shards_of in shards:
        draws = jax.random.uniform(jax.random.fold_in(jax.random.fold_in(own_key, 6), position), (shards_of,), jnp.float32, smallest / len(shards), high / len(shards))
        level = level * jnp.repeat(jnp.exp(draws), shape[position] // shards_of).reshape((-1,) + (1,) * (len(shape) - 1 - position))
    return level


def centred(stream_key, extent, scale, limit, pieces=(), kind=jnp.bfloat16):
    loudness = steps_of(stream_key, extent, pieces, -0.22, 0.18) if pieces else 1.0
    drawn = jax.random.normal(stream_key, extent, jnp.float32) * scale * loudness
    return jnp.minimum(jnp.maximum(drawn, -limit), limit).astype(kind)


def setup_inputs(seed: int = 0) -> dict:
    key_of = jax.random.split(jax.random.key(seed), 9)
    sources = centred(key_of[0], (2, LEAVES, S, P_SIZE), 1.0, 6.0, ((1, 256),), jnp.float32)
    leaf_slot = draw_leaf_slot(jax.random.fold_in(key_of[8], 71), 0)
    in_basis = centred(key_of[2], (LEAVES, 2, R, P_SIZE), (2 * P_SIZE) ** -0.5, 0.25, ((0, 256),), jnp.float32)
    butterfly = centred(key_of[3], (LEVELS, N_LEAF, 2, R, 2 * R), (4 * R) ** -0.5, 0.375, ((1, 256),), jnp.float32)
    out_basis = centred(key_of[4], (LEAVES, 2, R, P_SIZE), (2 * R) ** -0.5, 0.5, ((0, 256),), jnp.float32)
    near_pairs = draw_near_pairs(jax.random.fold_in(key_of[8], 71), 0)
    near_count = draw_near_count(jax.random.fold_in(key_of[8], 71), 0)
    near_blocks = centred(key_of[7], (NEAR_TOTAL, 2, P_SIZE, P_SIZE), (2 * P_SIZE) ** -0.5, 0.25, ((0, 256),), jnp.float32)
    return {"sources": sources, "leaf_slot": leaf_slot, "in_basis": in_basis, "butterfly": butterfly, "out_basis": out_basis, "near_pairs": near_pairs, "near_count": near_count, "near_blocks": near_blocks}


HIGH = lax.Precision.HIGHEST


def complex_panel(blocks, panel):
    w_real = blocks[:, :, :R]
    w_imag = blocks[:, :, R:]
    real_part = jnp.einsum('nrk,nkj->nrj', w_real, panel[0], precision=HIGH) - jnp.einsum('nrk,nkj->nrj', w_imag, panel[1], precision=HIGH)
    imag_part = jnp.einsum('nrk,nkj->nrj', w_real, panel[1], precision=HIGH) + jnp.einsum('nrk,nkj->nrj', w_imag, panel[0], precision=HIGH)
    return jnp.stack([real_part, imag_part])


def reference(sources, leaf_slot, in_basis, butterfly, out_basis, near_pairs, near_count, near_blocks):
    coeff_real = jnp.einsum('lrp,lsp->lrs', in_basis[:, 0], sources[0], precision=HIGH) - jnp.einsum('lrp,lsp->lrs', in_basis[:, 1], sources[1], precision=HIGH)
    coeff_imag = jnp.einsum('lrp,lsp->lrs', in_basis[:, 0], sources[1], precision=HIGH) + jnp.einsum('lrp,lsp->lrs', in_basis[:, 1], sources[0], precision=HIGH)
    coeff = jnp.stack([coeff_real, coeff_imag])
    panel = coeff.reshape(2, N_LEAF, LEAF_DEV, R, S).transpose(0, 1, 3, 2, 4).reshape(2, N_LEAF, R, LEAF_DEV * S)
    devices = jnp.arange(N_LEAF, dtype=jnp.int32)
    for level_bit in range(LEVELS):
        partner = jnp.bitwise_xor(devices, jnp.int32(1 << level_bit))
        other = panel[:, partner]
        panel = complex_panel(butterfly[level_bit, :, 0], panel) + complex_panel(butterfly[level_bit, :, 1], other)
    final = panel.reshape(2, N_LEAF, R, LEAF_DEV, S).transpose(0, 1, 3, 2, 4).reshape(2, LEAVES, R, S)
    far_real = jnp.einsum('lrs,lrp->lsp', final[0], out_basis[:, 0], precision=HIGH) - jnp.einsum('lrs,lrp->lsp', final[1], out_basis[:, 1], precision=HIGH)
    far_imag = jnp.einsum('lrs,lrp->lsp', final[1], out_basis[:, 0], precision=HIGH) + jnp.einsum('lrs,lrp->lsp', final[0], out_basis[:, 1], precision=HIGH)
    slots_all = jnp.arange(NEAR_TOTAL, dtype=jnp.int32)
    live = (slots_all % NEAR_DEV) < near_count[slots_all // NEAR_DEV]
    src_slot = leaf_slot[near_pairs[:, 0]].astype(jnp.int32)
    tgt_slot = leaf_slot[near_pairs[:, 1]].astype(jnp.int32)
    picked = sources[:, src_slot]
    term_real = jnp.einsum('bpq,bsq->bsp', near_blocks[:, 0], picked[0], precision=HIGH) - jnp.einsum('bpq,bsq->bsp', near_blocks[:, 1], picked[1], precision=HIGH)
    term_imag = jnp.einsum('bpq,bsq->bsp', near_blocks[:, 0], picked[1], precision=HIGH) + jnp.einsum('bpq,bsq->bsp', near_blocks[:, 1], picked[0], precision=HIGH)
    weight = live.astype(jnp.float32)[:, None, None]
    near_real = jnp.zeros_like(far_real).at[tgt_slot].add(term_real * weight)
    near_imag = jnp.zeros_like(far_imag).at[tgt_slot].add(term_imag * weight)
    return jnp.stack([far_real + near_real, far_imag + near_imag])
```

```python
import functools

import jax
import jax.numpy as jnp
from jax import lax
from jax.experimental import pallas as pl
from jax.experimental.pallas import tpu as pltpu
from jax.sharding import PartitionSpec as P

MESH = pl.DeviceIdType.MESH
F32, BF16 = jnp.float32, jnp.bfloat16
GROUPS = ((0,), (1, 2), (3, 4), (5,), (6, 7))
CHUNKS = 2
HALO = 4


def masks_of(group):
    if len(group) == 1:
        return (1 << group[0],)
    low, high = 1 << group[0], 1 << group[1]
    return (low, high, low | high)


MASKS = tuple(masks_of(g) for g in GROUPS)
FIRST = tuple(sum(len(m) for m in MASKS[:i]) for i in range(len(MASKS)))
N_RECV = sum(len(m) for m in MASKS)
W_FIRST = tuple(sum(len(m) + 1 for m in MASKS[:i]) for i in range(len(MASKS)))
N_W = N_RECV + len(MASKS)
DOUBLE = tuple(i for i, g in enumerate(GROUPS) if len(g) == 2)


def split(x):
    high = x.astype(BF16)
    return high, (x - high.astype(F32)).astype(BF16)


def dot(a, b):
    return jnp.dot(a, b, preferred_element_type=F32)


def dot_nt(a, b):
    return lax.dot_general(a, b, (((1,), (1,)), ((), ())), preferred_element_type=F32)


def kernel(src_hbm, slot_hbm, inb_hbm, bf_hbm, outb_hbm, pairs_hbm, count_hbm, near_hbm, out_ref,
           src, inb, bf, outb, near, slots, pairs, count, bp, pack, halo, w, wtmp, obf, nacc, panel, recv,
           load_sem, in_sem, bp_send, bp_recv, halo_send, halo_recv, p_send, p_recv):
    n = lax.axis_size("leaf")
    me = lax.axis_index("leaf")
    nxt, prv = lax.rem(me + 1, n), lax.rem(me + n - 1, n)
    leaves = src.shape[1]
    base = me * leaves
    rows = panel.shape[1]
    part = rows // CHUNKS
    rank2 = panel.shape[2]
    rank = rank2 // 2

    barrier = pltpu.get_barrier_semaphore()
    partners = [me ^ m for ms in MASKS for m in ms] + [nxt, prv]
    for p in partners:
        pl.semaphore_signal(barrier, inc=1, device_id=(p,), device_id_type=MESH)

    loads = [
        pltpu.make_async_copy(bf_hbm, bf, load_sem.at[0]),
        pltpu.make_async_copy(src_hbm, src, load_sem.at[1]),
        pltpu.make_async_copy(slot_hbm, slots, load_sem.at[2]),
        pltpu.make_async_copy(pairs_hbm, pairs, load_sem.at[3]),
        pltpu.make_async_copy(count_hbm, count, load_sem.at[4]),
        pltpu.make_async_copy(outb_hbm, outb, load_sem.at[5]),
        pltpu.make_async_copy(near_hbm, near, load_sem.at[6]),
    ]
    per = leaves // in_sem.shape[0]
    in_loads = [
        pltpu.make_async_copy(inb_hbm.at[pl.ds(i * per, per)], inb.at[pl.ds(i * per, per)], in_sem.at[i])
        for i in range(in_sem.shape[0])
    ]
    for c in loads[:2] + in_loads + loads[2:]:
        c.start()

    lane = lax.broadcasted_iota(jnp.int32, (1, rank2), 1)
    sign = jnp.where(lane < rank, 1.0, -1.0).astype(F32)

    def real_form(block):
        return jnp.concatenate([block * sign, pltpu.roll(block, rank, 1)], axis=0).T

    def weights(t):
        row = jnp.concatenate(split(t), axis=1)
        return jnp.concatenate([row, row], axis=0)

    def times(x, wide):
        y = dot(jnp.concatenate(split(x), axis=1), wide)
        return y[:, :rank2] + y[:, rank2:]

    def prepare_single(i):
        b = GROUPS[i][0]
        for k in range(2):
            w[W_FIRST[i] + k] = weights(real_form(bf[2 * b + k]))

    def prepare_double(i):
        a, b = GROUPS[i]
        d = DOUBLE.index(i)
        for k in range(2):
            if k == 0:
                lower = [bf[2 * a], bf[2 * a + 1]]
            else:
                bp_copy[d].wait_recv()
                lower = [bp[d, 0], bp[d, 1]]
            wtmp[...] = weights(real_form(bf[2 * b + k]))
            t = times(jnp.concatenate([real_form(x) for x in lower], axis=0), wtmp[...])
            w[W_FIRST[i] + 2 * k] = weights(t[:rank2])
            w[W_FIRST[i] + 2 * k + 1] = weights(t[rank2:])

    def panel_copies(i, c):
        sl = pl.ds(c * part, part)
        return [
            pltpu.make_async_remote_copy(
                src_ref=panel.at[i, sl], dst_ref=recv.at[FIRST[i] + e, sl],
                send_sem=p_send.at[FIRST[i] + e, c], recv_sem=p_recv.at[FIRST[i] + e, c],
                device_id=(me ^ m,), device_id_type=MESH)
            for e, m in enumerate(MASKS[i])
        ]

    copies = [[panel_copies(i, c) for c in range(CHUNKS)] for i in range(len(GROUPS))]
    bp_copy = [
        pltpu.make_async_remote_copy(
            src_ref=bf.at[pl.ds(2 * GROUPS[i][0], 2)], dst_ref=bp.at[d],
            send_sem=bp_send.at[d], recv_sem=bp_recv.at[d],
            device_id=(me ^ (1 << GROUPS[i][1]),), device_id_type=MESH)
        for d, i in enumerate(DOUBLE)
    ]
    halo_copy = [
        pltpu.make_async_remote_copy(
            src_ref=pack.at[pl.ds(h * HALO, HALO)], dst_ref=halo.at[pl.ds(h * HALO, HALO)],
            send_sem=halo_send.at[h], recv_sem=halo_recv.at[h], device_id=(to,), device_id_type=MESH)
        for h, to in ((0, nxt), (1, prv))
    ]

    loads[0].wait()
    prepare_single(0)
    loads[1].wait()

    def coeff(j, carry):
        x = jnp.concatenate([src[0, j], src[1, j]], axis=0)
        y = dot_nt(jnp.concatenate(split(x), axis=0), jnp.concatenate(split(inb[j]), axis=0))
        y = y[:16] + y[16:]
        y = y[:, :rank2] + y[:, rank2:]
        panel[0, pl.ds(pl.multiple_of(j * 8, 8), 8)] = y[:8] - sign * pltpu.roll(y[8:], rank, 1)
        return carry

    waited = 0
    for c in range(CHUNKS):
        count_in = (c + 1) * len(in_loads) // CHUNKS
        for i in range(waited, count_in):
            in_loads[i].wait()
            lax.fori_loop(i * per, (i + 1) * per, coeff, 0, unroll=True)
        waited = count_in
        if c == 0:
            pl.semaphore_wait(barrier, len(partners))
        for cp in copies[0][c]:
            cp.start()

    for cp in bp_copy:
        cp.start()
    loads[2].wait()
    for h in range(2):
        for i in range(HALO):
            leaf = base + (leaves - HALO + i if h == 0 else i)
            where = jnp.clip(slots[leaf] - base, 0, leaves - 1)
            pack[h * HALO + i] = src[:, where]
        halo_copy[h].start()

    def prepare_out(j, carry):
        high, low = split(outb[j])
        obf[j, pl.ds(0, rank2)] = high
        obf[j, pl.ds(rank2, rank2)] = low
        return carry

    leaf_iota = lax.broadcasted_iota(jnp.int32, (leaves, 1, 1), 0)

    def near_term(k, carry):
        a, t = pairs[0, k], pairs[1, k]
        own = jnp.clip(slots[a] - base, 0, leaves - 1)
        off = jnp.clip(jnp.where(a < base, a - base + HALO, a - base - leaves + HALO), 0, 2 * HALO - 1)
        inside = jnp.logical_and(a >= base, a < base + leaves)
        x = jnp.where(inside, src[:, own], halo[off]).reshape(16, -1)
        high, low = split(x)
        both = jnp.concatenate([high, low], axis=0)
        y = []
        for q in range(2):
            bh, bl = split(near[k, q])
            yh, yl = dot_nt(both, bh), dot_nt(high, bl)
            y.append(yh[:16] + yh[16:] + yl)
        hit = jnp.logical_and(leaf_iota == slots[t] - base, k < count[0])
        nacc[0] += jnp.where(hit, (y[0][:8] - y[1][8:])[None], 0.0)
        nacc[1] += jnp.where(hit, (y[0][8:] + y[1][:8])[None], 0.0)
        return carry

    def background(i):
        if i == 0:
            prepare_single(3)
            loads[5].wait()
            lax.fori_loop(0, leaves // 4, prepare_out, 0)
        if i == 1:
            prepare_double(1)
            prepare_double(2)
        if i == 2:
            prepare_double(4)
            lax.fori_loop(leaves // 4, leaves, prepare_out, 0)
            loads[3].wait()
            loads[4].wait()
            loads[6].wait()
            nacc[...] = jnp.zeros_like(nacc)
            for cp in halo_copy:
                cp.wait_recv()
        if i == 3:
            lax.fori_loop(0, 3, near_term, 0)
        if i == 4:
            lax.fori_loop(3, 8, near_term, 0)

    last = len(GROUPS) - 1
    for i in range(len(GROUPS)):
        own = [None] * CHUNKS
        if i in (0, 3):
            own = [times(panel[i, pl.ds(c * part, part)], w[W_FIRST[i]]) for c in range(CHUNKS)]
        background(i)
        if i not in (0, 3):
            own = [times(panel[i, pl.ds(c * part, part)], w[W_FIRST[i]]) for c in range(CHUNKS)]
        for c in range(CHUNKS):
            sl = pl.ds(c * part, part)
            acc = own[c]
            for e, cp in enumerate(copies[i][c]):
                cp.wait_recv()
                acc = acc + times(recv[FIRST[i] + e, sl], w[W_FIRST[i] + 1 + e])
            if i < last:
                panel[i + 1, sl] = acc
                for cp in copies[i + 1][c]:
                    cp.start()
            else:
                for j in range(c * leaves // CHUNKS, (c + 1) * leaves // CHUNKS):
                    r = (j - c * leaves // CHUNKS) * 8
                    x = acc[r:r + 8]
                    high, low = split(jnp.concatenate([x * sign, pltpu.roll(x, rank, 1)], axis=0))
                    lhs = jnp.concatenate(
                        [jnp.concatenate([high, high], axis=1), jnp.concatenate([low, low], axis=1)], axis=0)
                    y = dot(lhs, obf[j])
                    y = y[:16] + y[16:]
                    out_ref[0, j] = y[:8] + nacc[0, j]
                    out_ref[1, j] = y[8:] + nacc[1, j]

    for row in copies:
        for chunk in row:
            for cp in chunk:
                cp.wait_send()
    for cp in bp_copy + halo_copy:
        cp.wait_send()


def body(sources, leaf_slot, in_basis, butterfly, out_basis, near_pairs, near_count, near_blocks):
    leaves, s, size = sources.shape[1:]
    rank = in_basis.shape[2]
    levels = butterfly.shape[0]
    slots = near_pairs.shape[0]
    rows = leaves * s
    any_spec = pl.BlockSpec(memory_space=pl.ANY)
    dma = pltpu.SemaphoreType.DMA
    return pl.pallas_call(
        kernel,
        out_shape=pltpu.VMEM(sources.shape, F32),
        in_specs=[any_spec] * 8,
        out_specs=pl.BlockSpec(memory_space=pltpu.VMEM),
        scratch_shapes=[
            pltpu.VMEM(sources.shape, F32),
            pltpu.VMEM((leaves, 2 * rank, size), F32),
            pltpu.VMEM((2 * levels, rank, 2 * rank), F32),
            pltpu.VMEM((leaves, 2 * rank, size), F32),
            pltpu.VMEM(near_blocks.shape, F32),
            pltpu.SMEM(leaf_slot.shape, jnp.int32),
            pltpu.SMEM(near_pairs.shape[::-1], jnp.int32),
            pltpu.SMEM(near_count.shape, jnp.int32),
            pltpu.VMEM((len(DOUBLE), 2, rank, 2 * rank), F32),
            pltpu.VMEM((2 * HALO, 2, s, size), F32),
            pltpu.VMEM((2 * HALO, 2, s, size), F32),
            pltpu.VMEM((N_W, 4 * rank, 4 * rank), BF16),
            pltpu.VMEM((4 * rank, 4 * rank), BF16),
            pltpu.VMEM((leaves, 4 * rank, size), BF16),
            pltpu.VMEM(sources.shape, F32),
            pltpu.VMEM((len(GROUPS), rows, 2 * rank), F32),
            pltpu.VMEM((N_RECV, rows, 2 * rank), F32),
            dma((7,)),
            dma((4,)),
            dma((len(DOUBLE),)),
            dma((len(DOUBLE),)),
            dma((2,)),
            dma((2,)),
            dma((N_RECV, CHUNKS)),
            dma((N_RECV, CHUNKS)),
        ],
        compiler_params=pltpu.CompilerParams(
            collective_id=0, has_side_effects=True, vmem_limit_bytes=60 * 1024 * 1024),
        name="butterfly",
    )(sources, leaf_slot, in_basis.reshape(leaves, 2 * rank, size),
      butterfly.reshape(2 * levels, rank, 2 * rank), out_basis.reshape(leaves, 2 * rank, size),
      near_pairs.T, near_count, near_blocks)


def solution(mesh):
    in_specs = (
        P(None, "leaf", None, None),
        P(),
        P("leaf", None, None, None),
        P(None, "leaf", None, None, None),
        P("leaf", None, None, None),
        P("leaf", None),
        P("leaf"),
        P("leaf", None, None, None),
    )
    out_specs = P(None, "leaf", None, None)
    return jax.shard_map(body, mesh=mesh, in_specs=in_specs, out_specs=out_specs, check_vma=False)
```

```python
import functools

import jax
import jax.numpy as jnp
from jax import lax
from jax.experimental import pallas as pl
from jax.experimental.pallas import tpu as pltpu
from jax.sharding import PartitionSpec as P

MESH = pl.DeviceIdType.MESH
F32, BF16 = jnp.float32, jnp.bfloat16
GROUPS = ((0,), (1, 2), (3, 4), (5,), (6, 7))
CHUNK_LEAVES = (4, 4, 4, 4)
CHUNKS = len(CHUNK_LEAVES)
START = tuple(sum(CHUNK_LEAVES[:c]) for c in range(CHUNKS + 1))
HALO = 4


def masks_of(group):
    if len(group) == 1:
        return (1 << group[0],)
    low, high = 1 << group[0], 1 << group[1]
    return (low, high, low | high)


MASKS = tuple(masks_of(g) for g in GROUPS)
FIRST = tuple(sum(len(m) for m in MASKS[:i]) for i in range(len(MASKS)))
N_RECV = sum(len(m) for m in MASKS)
W_FIRST = tuple(sum(len(m) + 1 for m in MASKS[:i]) for i in range(len(MASKS)))
N_W = N_RECV + len(MASKS)
DOUBLE = tuple(i for i, g in enumerate(GROUPS) if len(g) == 2)


def split(x):
    high = x.astype(BF16)
    return high, (x - high.astype(F32)).astype(BF16)


def dot(a, b):
    return jnp.dot(a, b, preferred_element_type=F32)


def dot_nt(a, b):
    return lax.dot_general(a, b, (((1,), (1,)), ((), ())), preferred_element_type=F32)


def kernel(src_hbm, slot_hbm, inb_hbm, bf_hbm, outb_hbm, pairs_hbm, count_hbm, near_hbm, out_ref,
           src, inb, bf, outb, near, slots, pairs, count, bp, pack, halo, w, wtmp, obf, nacc, panel, recv,
           load_sem, in_sem, bp_send, bp_recv, halo_send, halo_recv, p_send, p_recv, known):
    n = lax.axis_size("leaf")
    me = lax.axis_index("leaf")
    nxt, prv = lax.rem(me + 1, n), lax.rem(me + n - 1, n)
    leaves = src.shape[1]
    base = me * leaves
    width = panel.shape[1] // leaves
    rank2 = panel.shape[2]
    rank = rank2 // 2

    step = 1 << GROUPS[3][0]
    up, down = lax.rem(me + step, n), lax.rem(me + n - step, n)
    barrier = pltpu.get_barrier_semaphore()
    neighbours = [me ^ 1, me ^ 2, me ^ 4, me ^ 6, me ^ 8, me ^ 16, me ^ 24, up, down, nxt, prv]
    for p in neighbours:
        pl.semaphore_signal(barrier, inc=1, device_id=(p,), device_id_type=MESH)

    loads = [
        pltpu.make_async_copy(bf_hbm, bf, load_sem.at[0]),
        pltpu.make_async_copy(src_hbm, src, load_sem.at[1]),
        pltpu.make_async_copy(slot_hbm, slots, load_sem.at[2]),
        pltpu.make_async_copy(pairs_hbm, pairs, load_sem.at[3]),
        pltpu.make_async_copy(count_hbm, count, load_sem.at[4]),
        pltpu.make_async_copy(outb_hbm, outb, load_sem.at[5]),
        pltpu.make_async_copy(near_hbm, near, load_sem.at[6]),
    ]
    per = leaves // in_sem.shape[0]
    in_loads = [
        pltpu.make_async_copy(inb_hbm.at[pl.ds(i * per, per)], inb.at[pl.ds(i * per, per)], in_sem.at[i])
        for i in range(in_sem.shape[0])
    ]
    for c in [loads[0], loads[1]] + in_loads + loads[2:]:
        c.start()

    lane = lax.broadcasted_iota(jnp.int32, (1, rank2), 1)
    sign = jnp.where(lane < rank, 1.0, -1.0).astype(F32)

    def real_form(block):
        return jnp.concatenate([block * sign, pltpu.roll(block, rank, 1)], axis=0).T

    def weights(t):
        return jnp.concatenate(split(t), axis=1)

    def times(xs, wide):
        high, low = zip(*[split(x) for x in xs])
        y = dot(jnp.concatenate([jnp.concatenate(high, axis=1), jnp.concatenate(low, axis=1)], axis=0), wide)
        y = y[:, :rank2] + y[:, rank2:]
        return y[:y.shape[0] // 2] + y[y.shape[0] // 2:]

    def prepare_single(i):
        b = GROUPS[i][0]
        for k in range(2):
            w[W_FIRST[i] + k] = weights(real_form(bf[2 * b + k]))

    def prepare_double(i):
        a, b = GROUPS[i]
        d = DOUBLE.index(i)
        for k in range(2):
            if k == 0:
                lower = [bf[2 * a], bf[2 * a + 1]]
            else:
                bp_copy[d].wait_recv()
                lower = [bp[d, 0], bp[d, 1]]
            wtmp[...] = weights(real_form(bf[2 * b + k]))
            t = times([jnp.concatenate([real_form(x) for x in lower], axis=0)], wtmp[...])
            w[W_FIRST[i] + 2 * k] = weights(t[:rank2])
            w[W_FIRST[i] + 2 * k + 1] = weights(t[rank2:])

    def chunk(c):
        return pl.ds(START[c] * width, CHUNK_LEAVES[c] * width)

    def panel_copies(i, c):
        return [
            pltpu.make_async_remote_copy(
                src_ref=panel.at[i, chunk(c)], dst_ref=recv.at[FIRST[i] + e, chunk(c)],
                send_sem=p_send.at[0], recv_sem=p_recv.at[i, c],
                device_id=(me ^ m,), device_id_type=MESH)
            for e, m in enumerate(MASKS[i])
        ]

    def send(i, c):
        for cp in panel_copies(i, c)[::-1]:
            cp.start()

    def arrive(i, c):
        ref = recv.at[pl.ds(FIRST[i], len(MASKS[i])), chunk(c)]
        pltpu.make_async_copy(ref, ref, p_recv.at[i, c]).wait()

    bp_copy = [
        pltpu.make_async_remote_copy(
            src_ref=bf.at[pl.ds(2 * GROUPS[i][0], 2)], dst_ref=bp.at[d],
            send_sem=bp_send.at[0], recv_sem=bp_recv.at[d],
            device_id=(me ^ (1 << GROUPS[i][1]),), device_id_type=MESH)
        for d, i in enumerate(DOUBLE)
    ]
    halo_copy = [
        pltpu.make_async_remote_copy(
            src_ref=pack.at[pl.ds(h * HALO, HALO)], dst_ref=halo.at[pl.ds(h * HALO, HALO)],
            send_sem=halo_send.at[0], recv_sem=halo_recv.at[h], device_id=(to,), device_id_type=MESH)
        for h, to in ((0, nxt), (1, prv))
    ]

    def tell(k, to):
        pl.semaphore_signal(known.at[k], inc=1, device_id=(to,), device_id_type=MESH)

    loads[0].wait()
    pl.semaphore_wait(barrier, len(neighbours))
    bp_copy[0].start()
    bp_copy[1].start()
    loads[1].wait()

    def coeff(j, carry):
        x = jnp.concatenate([src[0, j], src[1, j]], axis=0)
        y = dot_nt(jnp.concatenate(split(x), axis=0), jnp.concatenate(split(inb[j]), axis=0))
        y = y[:16] + y[16:]
        y = y[:, :rank2] + y[:, rank2:]
        panel[0, pl.ds(pl.multiple_of(j * 8, 8), 8)] = y[:8] - sign * pltpu.roll(y[8:], rank, 1)
        return carry

    waited = 0
    for c in range(CHUNKS):
        count_in = -(-START[c + 1] // per)
        for i in range(waited, count_in):
            in_loads[i].wait()
        waited = count_in
        lax.fori_loop(START[c], START[c + 1], coeff, 0, unroll=True)
        send(0, c)

    tell(2, up)
    tell(2, down)
    prepare_single(0)

    def pack_halo():
        loads[2].wait()
        for h in range(2):
            for i in range(HALO):
                leaf = base + (leaves - HALO + i if h == 0 else i)
                where = jnp.clip(slots[leaf] - base, 0, leaves - 1)
                pack[h * HALO + i] = src[:, where]
            halo_copy[h].start()

    def prepare_out(j, carry):
        high, low = split(outb[j])
        obf[j, pl.ds(0, rank2)] = high
        obf[j, pl.ds(rank2, rank2)] = low
        return carry

    leaf_iota = lax.broadcasted_iota(jnp.int32, (leaves, 1, 1), 0)

    def near_term(k, carry):
        a, t = pairs[0, k], pairs[1, k]
        own = jnp.clip(slots[a] - base, 0, leaves - 1)
        off = jnp.clip(jnp.where(a < base, a - base + HALO, a - base - leaves + HALO), 0, 2 * HALO - 1)
        inside = jnp.logical_and(a >= base, a < base + leaves)
        x = jnp.where(inside, src[:, own], halo[off]).reshape(16, -1)
        high, low = split(x)
        both = jnp.concatenate([high, low], axis=0)
        y = []
        for q in range(2):
            bh, bl = split(near[k, q])
            yh, yl = dot_nt(both, bh), dot_nt(high, bl)
            y.append(yh[:16] + yh[16:] + yl)
        hit = jnp.logical_and(leaf_iota == slots[t] - base, k < count[0])
        nacc[0] += jnp.where(hit, (y[0][:8] - y[1][8:])[None], 0.0)
        nacc[1] += jnp.where(hit, (y[0][8:] + y[1][:8])[None], 0.0)
        return carry

    def background(i):
        if i == 0:
            prepare_single(3)
            pl.semaphore_wait(known.at[2], 2)
            tell(3, me ^ (1 << GROUPS[4][0]))
        if i == 1:
            prepare_double(1)
            prepare_double(2)
        if i == 2:
            pl.semaphore_wait(known.at[3], 1)
            bp_copy[2].start()
            pack_halo()
            loads[5].wait()
            lax.fori_loop(0, leaves, prepare_out, 0)
        if i == 4:
            prepare_double(4)
            loads[3].wait()
            loads[4].wait()
            loads[6].wait()
            nacc[...] = jnp.zeros_like(nacc)
            for cp in halo_copy:
                cp.wait_recv()
            lax.fori_loop(0, 8, near_term, 0)

    def far(acc, j, r):
        x = acc[r:r + width]
        high, low = split(jnp.concatenate([x * sign, pltpu.roll(x, rank, 1)], axis=0))
        lhs = jnp.concatenate(
            [jnp.concatenate([high, high], axis=1), jnp.concatenate([low, low], axis=1)], axis=0)
        y = dot(lhs, obf[j])
        y = y[:16] + y[16:]
        out_ref[0, j] = y[:8] + nacc[0, j]
        out_ref[1, j] = y[8:] + nacc[1, j]

    last = len(GROUPS) - 1
    for i in range(len(GROUPS)):
        background(i)
        blocks = len(MASKS[i]) + 1
        for c in range(CHUNKS):
            arrive(i, c)
            xs = [panel[i, chunk(c)]] + [recv[FIRST[i] + e, chunk(c)] for e in range(blocks - 1)]
            acc = times(xs, w[pl.ds(W_FIRST[i], blocks)].reshape(blocks * rank2, 2 * rank2))
            if i < last:
                panel[i + 1, chunk(c)] = acc
                send(i + 1, c)
            else:
                for j in range(START[c], START[c + 1]):
                    far(acc, j, (j - START[c]) * width)

    for ref, sem in ((recv, p_send), (bp, bp_send), (pack, halo_send)):
        pltpu.make_async_copy(ref, ref, sem.at[0]).wait()


def body(sources, leaf_slot, in_basis, butterfly, out_basis, near_pairs, near_count, near_blocks):
    leaves, s, size = sources.shape[1:]
    rank = in_basis.shape[2]
    levels = butterfly.shape[0]
    slots = near_pairs.shape[0]
    rows = leaves * s
    any_spec = pl.BlockSpec(memory_space=pltpu.HBM)
    dma = pltpu.SemaphoreType.DMA
    return pl.pallas_call(
        kernel,
        out_shape=pltpu.VMEM(sources.shape, F32),
        in_specs=[any_spec] * 8,
        out_specs=pl.BlockSpec(memory_space=pltpu.VMEM),
        scratch_shapes=[
            pltpu.VMEM(sources.shape, F32),
            pltpu.VMEM((leaves, 2 * rank, size), F32),
            pltpu.VMEM((2 * levels, rank, 2 * rank), F32),
            pltpu.VMEM((leaves, 2 * rank, size), F32),
            pltpu.VMEM(near_blocks.shape, F32),
            pltpu.SMEM(leaf_slot.shape, jnp.int32),
            pltpu.SMEM(near_pairs.shape[::-1], jnp.int32),
            pltpu.SMEM(near_count.shape, jnp.int32),
            pltpu.VMEM((len(DOUBLE), 2, rank, 2 * rank), F32),
            pltpu.VMEM((2 * HALO, 2, s, size), F32),
            pltpu.VMEM((2 * HALO, 2, s, size), F32),
            pltpu.VMEM((N_W, 2 * rank, 4 * rank), BF16),
            pltpu.VMEM((2 * rank, 4 * rank), BF16),
            pltpu.VMEM((leaves, 4 * rank, size), BF16),
            pltpu.VMEM(sources.shape, F32),
            pltpu.VMEM((len(GROUPS), rows, 2 * rank), F32),
            pltpu.VMEM((N_RECV, rows, 2 * rank), F32),
            dma((7,)),
            dma((4,)),
            dma((1,)),
            dma((len(DOUBLE),)),
            dma((1,)),
            dma((2,)),
            dma((1,)),
            dma((len(GROUPS), CHUNKS)),
            pltpu.SemaphoreType.REGULAR((4,)),
        ],
        compiler_params=pltpu.CompilerParams(
            collective_id=0, has_side_effects=True, vmem_limit_bytes=60 * 1024 * 1024),
        name="butterfly",
    )(sources, leaf_slot, in_basis.reshape(leaves, 2 * rank, size),
      butterfly.reshape(2 * levels, rank, 2 * rank), out_basis.reshape(leaves, 2 * rank, size),
      near_pairs.T, near_count, near_blocks)


def solution(mesh):
    in_specs = (
        P(None, "leaf", None, None),
        P(),
        P("leaf", None, None, None),
        P(None, "leaf", None, None, None),
        P("leaf", None, None, None),
        P("leaf", None),
        P("leaf"),
        P("leaf", None, None, None),
    )
    out_specs = P(None, "leaf", None, None)
    return jax.shard_map(body, mesh=mesh, in_specs=in_specs, out_specs=out_specs, check_vma=False)
```

```python
import functools

import jax
import jax.numpy as jnp
from jax import lax
from jax.experimental import pallas as pl
from jax.experimental.pallas import tpu as pltpu
from jax.sharding import PartitionSpec as P

MESH = pl.DeviceIdType.MESH
F32, BF16 = jnp.float32, jnp.bfloat16
GROUPS = ((0,), (1, 2), (3, 4))
CHUNK_LEAVES = (4, 4, 4, 4)
CHUNKS = len(CHUNK_LEAVES)
DIRECT = 2
START = tuple(sum(CHUNK_LEAVES[:c]) for c in range(CHUNKS + 1))
HALO = 4


def masks_of(group):
    if len(group) == 1:
        return (1 << group[0],)
    low, high = 1 << group[0], 1 << group[1]
    return (low, high, low | high)


Z1, Z2 = 3, 4
MASKS = tuple(masks_of(g) for g in GROUPS) + ((32,), (160, 128, 64, 192))
FIRST = tuple(sum(len(m) for m in MASKS[:i]) for i in range(len(MASKS)))
N_RECV = sum(len(m) for m in MASKS)
W_FIRST = tuple(sum(len(m) + 1 for m in MASKS[:i]) for i in range(len(GROUPS) + 1))
W_FAR, W_NEAR, W_OWN, W_LAST = (W_FIRST[-1] + 2 * i for i in range(4))
N_W = W_FIRST[-1] + 8
DOUBLE = tuple(i for i, g in enumerate(GROUPS) if len(g) == 2)


def split(x):
    high = x.astype(BF16)
    return high, (x - high.astype(F32)).astype(BF16)


def dot(a, b):
    return jnp.dot(a, b, preferred_element_type=F32)


def dot_nt(a, b):
    return lax.dot_general(a, b, (((1,), (1,)), ((), ())), preferred_element_type=F32)


def kernel(src_hbm, slot_hbm, inb_hbm, bf_hbm, outb_hbm, pairs_hbm, count_hbm, near_hbm, out_ref,
           src, inb, bf, outb, near, slots, pairs, count, bp, pack, halo, w, wtmp, obf, nacc, panel, recv,
           z_panel, z_own, m_out, m_in, b_in,
           load_sem, in_sem, bp_send, bp_recv, m_send, m_recv, halo_send, halo_recv, p_send, p_recv, known):
    n = lax.axis_size("leaf")
    me = lax.axis_index("leaf")
    nxt, prv = lax.rem(me + 1, n), lax.rem(me + n - 1, n)
    leaves = src.shape[1]
    base = me * leaves
    width = panel.shape[1] // leaves
    rank2 = panel.shape[2]
    rank = rank2 // 2

    step = MASKS[Z1][0]
    up, down = lax.rem(me + step, n), lax.rem(me + n - step, n)
    barrier = pltpu.get_barrier_semaphore()
    neighbours = [me ^ 1, me ^ 2, me ^ 4, me ^ 6, me ^ 8, me ^ 16, me ^ 24, up, down, nxt, prv]
    for p in neighbours:
        pl.semaphore_signal(barrier, inc=1, device_id=(p,), device_id_type=MESH)

    loads = [
        pltpu.make_async_copy(bf_hbm, bf, load_sem.at[0]),
        pltpu.make_async_copy(src_hbm, src, load_sem.at[1]),
        pltpu.make_async_copy(slot_hbm, slots, load_sem.at[2]),
        pltpu.make_async_copy(pairs_hbm, pairs, load_sem.at[3]),
        pltpu.make_async_copy(count_hbm, count, load_sem.at[4]),
        pltpu.make_async_copy(outb_hbm, outb, load_sem.at[5]),
        pltpu.make_async_copy(near_hbm, near, load_sem.at[6]),
    ]
    per = leaves // in_sem.shape[0]
    in_loads = [
        pltpu.make_async_copy(inb_hbm.at[pl.ds(i * per, per)], inb.at[pl.ds(i * per, per)], in_sem.at[i])
        for i in range(in_sem.shape[0])
    ]
    for c in [loads[1]] + in_loads[:1] + [loads[0]] + in_loads[1:] + loads[2:]:
        c.start()

    lane = lax.broadcasted_iota(jnp.int32, (1, rank2), 1)
    sign = jnp.where(lane < rank, 1.0, -1.0).astype(F32)

    def real_form(block):
        return jnp.concatenate([block * sign, pltpu.roll(block, rank, 1)], axis=0).T

    def weights(t):
        return jnp.concatenate(split(t), axis=1)

    def times(xs, wide):
        high, low = zip(*[split(x) for x in xs])
        y = dot(jnp.concatenate([jnp.concatenate(high, axis=1), jnp.concatenate(low, axis=1)], axis=0), wide)
        y = y[:, :rank2] + y[:, rank2:]
        return y[:y.shape[0] // 2] + y[y.shape[0] // 2:]

    def prepare_single(i):
        b = GROUPS[i][0]
        for k in range(2):
            w[W_FIRST[i] + k] = weights(real_form(bf[2 * b + k]))

    def prepare_double(i):
        a, b = GROUPS[i]
        d = DOUBLE.index(i)
        for k in range(2):
            if k == 0:
                lower = [bf[2 * a], bf[2 * a + 1]]
            else:
                bp_copy[d].wait_recv()
                lower = [bp[d, 0], bp[d, 1]]
            wtmp[...] = weights(real_form(bf[2 * b + k]))
            t = times([jnp.concatenate([real_form(x) for x in lower], axis=0)], wtmp[...])
            w[W_FIRST[i] + 2 * k] = weights(t[:rank2])
            w[W_FIRST[i] + 2 * k + 1] = weights(t[rank2:])

    def prepare_z_here():
        wtmp[...] = weights(real_form(bf[12]))
        t = times([jnp.concatenate([real_form(bf[10]), real_form(bf[11])], axis=0)], wtmp[...])
        w[W_FAR + 1] = weights(t[:rank2])
        w[W_OWN] = weights(t[:rank2])
        w[W_OWN + 1] = weights(t[rank2:])
        m_out[...] = t[rank2:]
        for k in range(2):
            w[W_LAST + k] = weights(real_form(bf[14 + k]))

    def prepare_z_there():
        m_copy[0].wait_recv()
        w[W_FAR] = weights(m_in[...])
        m_copy[1].wait_recv()
        wtmp[...] = weights(real_form(b_in[...]))
        t = times([jnp.concatenate([real_form(bf[10]), real_form(bf[11])], axis=0)], wtmp[...])
        for k in range(2):
            w[W_NEAR + k] = weights(t[k * rank2:(k + 1) * rank2])

    def chunk(c):
        return pl.ds(START[c] * width, CHUNK_LEAVES[c] * width)

    def copy_to(ref, i, e, c):
        return pltpu.make_async_remote_copy(
            src_ref=ref.at[chunk(c)], dst_ref=recv.at[FIRST[i] + e, chunk(c)],
            send_sem=p_send.at[int(i == Z2 and e == 0)], recv_sem=p_recv.at[i, c],
            device_id=(me ^ MASKS[i][e],), device_id_type=MESH)

    def send(i, c):
        for e in range(len(MASKS[i]))[::-1]:
            copy_to(panel.at[i], i, e, c).start()

    def arrive(i, c):
        skip = int(i == Z2 and c < DIRECT)
        ref = recv.at[pl.ds(FIRST[i] + skip, len(MASKS[i]) - skip), chunk(c)]
        pltpu.make_async_copy(ref, ref, p_recv.at[i, c]).wait()

    bp_copy = [
        pltpu.make_async_remote_copy(
            src_ref=bf.at[pl.ds(2 * GROUPS[i][0], 2)], dst_ref=bp.at[d],
            send_sem=bp_send.at[0], recv_sem=bp_recv.at[d],
            device_id=(me ^ (1 << GROUPS[i][1]),), device_id_type=MESH)
        for d, i in enumerate(DOUBLE)
    ]
    m_copy = [
        pltpu.make_async_remote_copy(
            src_ref=ref, dst_ref=to, send_sem=m_send.at[k], recv_sem=m_recv.at[k],
            device_id=(me ^ m,), device_id_type=MESH)
        for k, (ref, to, m) in enumerate(((m_out, m_in, 32), (bf.at[13], b_in, 64)))
    ]
    halo_copy = [
        pltpu.make_async_remote_copy(
            src_ref=pack.at[pl.ds(h * HALO, HALO)], dst_ref=halo.at[pl.ds(h * HALO, HALO)],
            send_sem=halo_send.at[0], recv_sem=halo_recv.at[h], device_id=(to,), device_id_type=MESH)
        for h, to in ((0, nxt), (1, prv))
    ]

    def tell(k, to):
        pl.semaphore_signal(known.at[k], inc=1, device_id=(to,), device_id_type=MESH)

    loads[1].wait()

    def coeff(j, carry):
        x = jnp.concatenate([src[0, j], src[1, j]], axis=0)
        y = dot_nt(jnp.concatenate(split(x), axis=0), jnp.concatenate(split(inb[j]), axis=0))
        y = y[:16] + y[16:]
        y = y[:, :rank2] + y[:, rank2:]
        panel[0, pl.ds(pl.multiple_of(j * 8, 8), 8)] = y[:8] - sign * pltpu.roll(y[8:], rank, 1)
        return carry

    waited = 0
    for c in range(CHUNKS):
        count_in = -(-START[c + 1] // per)
        for i in range(waited, count_in):
            in_loads[i].wait()
        waited = count_in
        lax.fori_loop(START[c], START[c + 1], coeff, 0, unroll=True)
        if c == 0:
            pl.semaphore_wait(barrier, len(neighbours))
        send(0, c)
        if c == 0:
            loads[0].wait()
            bp_copy[0].start()
            bp_copy[1].start()

    tell(2, up)
    tell(2, down)
    prepare_single(0)

    def pack_halo():
        loads[2].wait()
        for h in range(2):
            for i in range(HALO):
                leaf = base + (leaves - HALO + i if h == 0 else i)
                where = jnp.clip(slots[leaf] - base, 0, leaves - 1)
                pack[h * HALO + i] = src[:, where]
            halo_copy[h].start()

    def prepare_out(j, carry):
        high, low = split(outb[j])
        obf[j, pl.ds(0, rank2)] = high
        obf[j, pl.ds(rank2, rank2)] = low
        return carry

    leaf_iota = lax.broadcasted_iota(jnp.int32, (leaves, 1, 1), 0)

    def near_term(k, carry):
        a, t = pairs[0, k], pairs[1, k]
        own = jnp.clip(slots[a] - base, 0, leaves - 1)
        off = jnp.clip(jnp.where(a < base, a - base + HALO, a - base - leaves + HALO), 0, 2 * HALO - 1)
        inside = jnp.logical_and(a >= base, a < base + leaves)
        x = jnp.where(inside, src[:, own], halo[off]).reshape(16, -1)
        high, low = split(x)
        both = jnp.concatenate([high, low], axis=0)
        y = []
        for q in range(2):
            bh, bl = split(near[k, q])
            yh, yl = dot_nt(both, bh), dot_nt(high, bl)
            y.append(yh[:16] + yh[16:] + yl)
        hit = jnp.logical_and(leaf_iota == slots[t] - base, k < count[0])
        nacc[0] += jnp.where(hit, (y[0][:8] - y[1][8:])[None], 0.0)
        nacc[1] += jnp.where(hit, (y[0][8:] + y[1][:8])[None], 0.0)
        return carry

    def background(i):
        if i == 0:
            pl.semaphore_wait(known.at[2], 2)
            tell(3, me ^ 64)
            tell(3, me ^ 192)
        if i == 1:
            prepare_double(1)
            prepare_z_here()
            m_copy[0].start()
            m_copy[1].start()
        if i == 2:
            pack_halo()
            prepare_double(2)
            pl.semaphore_wait(known.at[3], 2)
            prepare_z_there()
        if i == 3:
            loads[5].wait()
            lax.fori_loop(0, leaves, prepare_out, 0)
        if i == 4:
            loads[3].wait()
            loads[4].wait()
            loads[6].wait()
            nacc[...] = jnp.zeros_like(nacc)
            for cp in halo_copy:
                cp.wait_recv()
            lax.fori_loop(0, 8, near_term, 0)

    def far(acc, j, r):
        x = acc[r:r + width]
        high, low = split(jnp.concatenate([x * sign, pltpu.roll(x, rank, 1)], axis=0))
        lhs = jnp.concatenate(
            [jnp.concatenate([high, high], axis=1), jnp.concatenate([low, low], axis=1)], axis=0)
        y = dot(lhs, obf[j])
        y = y[:16] + y[16:]
        out_ref[0, j] = y[:8] + nacc[0, j]
        out_ref[1, j] = y[8:] + nacc[1, j]

    def stacked(first, blocks):
        return w[pl.ds(first, blocks)].reshape(blocks * rank2, 2 * rank2)

    def got(i, e, c):
        return recv[FIRST[i] + e, chunk(c)]

    for i in range(len(GROUPS)):
        background(i)
        blocks = len(MASKS[i]) + 1
        for c in range(CHUNKS):
            arrive(i, c)
            xs = [panel[i, chunk(c)]] + [got(i, e, c) for e in range(blocks - 1)]
            acc = times(xs, stacked(W_FIRST[i], blocks))
            panel[i + 1, chunk(c)] = acc
            send(i + 1, c)
            if i + 1 == Z1 and c >= DIRECT:
                for k in (1, 0):
                    z_panel[k, chunk(c)] = times([acc], w[W_FAR + k])
                    copy_to(z_panel.at[k], Z2, k, c).start()

    background(Z1)
    for c in range(CHUNKS):
        arrive(Z1, c)
        xs = [panel[Z1, chunk(c)], got(Z1, 0, c)]
        if c < DIRECT:
            z_panel[1, chunk(c)] = times(xs, stacked(W_OWN, 2))
            copy_to(z_panel.at[1], Z2, 1, c).start()
        z_panel[2, chunk(c)] = times(xs, stacked(W_NEAR, 2))
        for e in (2, 3):
            copy_to(z_panel.at[2], Z2, e, c).start()
        if c >= DIRECT:
            z_own[chunk(c)] = times(xs, stacked(W_OWN, 2))

    background(Z2)
    for c in range(CHUNKS):
        arrive(Z2, c)
        here, there = z_panel[1, chunk(c)] if c < DIRECT else z_own[chunk(c)], got(Z2, 1, c) + got(Z2, 3, c)
        if c >= DIRECT:
            there = there + got(Z2, 0, c)
        xs = [here + got(Z2, 2, c), there]
        acc = times(xs, stacked(W_LAST, 2))
        for j in range(START[c], START[c + 1]):
            far(acc, j, (j - START[c]) * width)

    for cp in m_copy:
        cp.wait_send()
    skipped = FIRST[Z2]
    for ref, sem in ((recv.at[pl.ds(0, skipped)], p_send.at[0]), (recv.at[pl.ds(skipped + 1, 3)], p_send.at[0]),
                     (bp, bp_send.at[0]), (pack, halo_send.at[0])):
        pltpu.make_async_copy(ref, ref, sem).wait()
    if DIRECT < CHUNKS:
        ref = recv.at[skipped, pl.ds(START[DIRECT] * width, (leaves - START[DIRECT]) * width)]
        pltpu.make_async_copy(ref, ref, p_send.at[1]).wait()


def body(sources, leaf_slot, in_basis, butterfly, out_basis, near_pairs, near_count, near_blocks):
    leaves, s, size = sources.shape[1:]
    rank = in_basis.shape[2]
    levels = butterfly.shape[0]
    slots = near_pairs.shape[0]
    rows = leaves * s
    any_spec = pl.BlockSpec(memory_space=pltpu.HBM)
    dma = pltpu.SemaphoreType.DMA
    return pl.pallas_call(
        kernel,
        out_shape=pltpu.VMEM(sources.shape, F32),
        in_specs=[any_spec] * 8,
        out_specs=pl.BlockSpec(memory_space=pltpu.VMEM),
        scratch_shapes=[
            pltpu.VMEM(sources.shape, F32),
            pltpu.VMEM((leaves, 2 * rank, size), F32),
            pltpu.VMEM((2 * levels, rank, 2 * rank), F32),
            pltpu.VMEM((leaves, 2 * rank, size), F32),
            pltpu.VMEM(near_blocks.shape, F32),
            pltpu.SMEM(leaf_slot.shape, jnp.int32),
            pltpu.SMEM(near_pairs.shape[::-1], jnp.int32),
            pltpu.SMEM(near_count.shape, jnp.int32),
            pltpu.VMEM((len(DOUBLE), 2, rank, 2 * rank), F32),
            pltpu.VMEM((2 * HALO, 2, s, size), F32),
            pltpu.VMEM((2 * HALO, 2, s, size), F32),
            pltpu.VMEM((N_W, 2 * rank, 4 * rank), BF16),
            pltpu.VMEM((2 * rank, 4 * rank), BF16),
            pltpu.VMEM((leaves, 4 * rank, size), BF16),
            pltpu.VMEM(sources.shape, F32),
            pltpu.VMEM((Z1 + 1, rows, 2 * rank), F32),
            pltpu.VMEM((N_RECV, rows, 2 * rank), F32),
            pltpu.VMEM((3, rows, 2 * rank), F32),
            pltpu.VMEM((rows, 2 * rank), F32),
            pltpu.VMEM((2 * rank, 2 * rank), F32),
            pltpu.VMEM((2 * rank, 2 * rank), F32),
            pltpu.VMEM((rank, 2 * rank), F32),
            dma((7,)),
            dma((4,)),
            dma((1,)),
            dma((len(DOUBLE),)),
            dma((2,)),
            dma((2,)),
            dma((1,)),
            dma((2,)),
            dma((2,)),
            dma((len(MASKS), CHUNKS)),
            pltpu.SemaphoreType.REGULAR((4,)),
        ],
        compiler_params=pltpu.CompilerParams(
            collective_id=0, has_side_effects=True, vmem_limit_bytes=60 * 1024 * 1024),
        name="butterfly",
    )(sources, leaf_slot, in_basis.reshape(leaves, 2 * rank, size),
      butterfly.reshape(2 * levels, rank, 2 * rank), out_basis.reshape(leaves, 2 * rank, size),
      near_pairs.T, near_count, near_blocks)


def solution(mesh):
    in_specs = (
        P(None, "leaf", None, None),
        P(),
        P("leaf", None, None, None),
        P(None, "leaf", None, None, None),
        P("leaf", None, None, None),
        P("leaf", None),
        P("leaf"),
        P("leaf", None, None, None),
    )
    out_specs = P(None, "leaf", None, None)
    return jax.shard_map(body, mesh=mesh, in_specs=in_specs, out_specs=out_specs, check_vma=False)
```

```python
import functools

import jax
import jax.numpy as jnp
from jax import lax
from jax.experimental import pallas as pl
from jax.experimental.pallas import tpu as pltpu
from jax.sharding import PartitionSpec as P

MESH = pl.DeviceIdType.MESH
F32, BF16 = jnp.float32, jnp.bfloat16
GROUPS = ((0,), (1, 2), (3, 4))
CHUNK_LEAVES = (4, 4, 4, 4)
CHUNKS = len(CHUNK_LEAVES)
DIRECT = 2
START = tuple(sum(CHUNK_LEAVES[:c]) for c in range(CHUNKS + 1))
HALO = 4


def masks_of(group):
    if len(group) == 1:
        return (1 << group[0],)
    low, high = 1 << group[0], 1 << group[1]
    return (low, high, low | high)


Z1, Z2 = 3, 4
MASKS = tuple(masks_of(g) for g in GROUPS) + ((32,), (160, 128, 64, 192))
FIRST = tuple(sum(len(m) for m in MASKS[:i]) for i in range(len(MASKS)))
N_RECV = sum(len(m) for m in MASKS)
W_FIRST = tuple(sum(len(m) + 1 for m in MASKS[:i]) for i in range(len(GROUPS) + 1))
W_FAR, W_NEAR, W_OWN, W_LAST = (W_FIRST[-1] + 2 * i for i in range(4))
N_W = W_FIRST[-1] + 8
DOUBLE = tuple(i for i, g in enumerate(GROUPS) if len(g) == 2)


def split(x):
    high = x.astype(BF16)
    return high, (x - high.astype(F32)).astype(BF16)


def dot(a, b):
    return jnp.dot(a, b, preferred_element_type=F32)


def dot_nt(a, b):
    return lax.dot_general(a, b, (((1,), (1,)), ((), ())), preferred_element_type=F32)


def kernel(src_hbm, slot_hbm, inb_hbm, bf_hbm, outb_hbm, pairs_hbm, count_hbm, near_hbm, out_ref,
           src, inb, bf, outb, near, slots, pairs, count, bp, pack, halo, w, wtmp, obf, nacc, panel, recv,
           z_panel, z_own, m_out, m_in, b_in,
           load_sem, in_sem, bp_send, bp_recv, m_send, m_recv, halo_send, halo_recv, p_send, p_recv, known):
    n = lax.axis_size("leaf")
    me = lax.axis_index("leaf")
    nxt, prv = lax.rem(me + 1, n), lax.rem(me + n - 1, n)
    leaves = src.shape[1]
    base = me * leaves
    width = panel.shape[1] // leaves
    rank2 = panel.shape[2]
    rank = rank2 // 2

    step = MASKS[Z1][0]
    up, down = lax.rem(me + step, n), lax.rem(me + n - step, n)
    barrier = pltpu.get_barrier_semaphore()
    neighbours = [me ^ 1, me ^ 2, me ^ 4, me ^ 6, me ^ 8, me ^ 16, me ^ 24, up, down, nxt, prv]
    for p in neighbours:
        pl.semaphore_signal(barrier, inc=1, device_id=(p,), device_id_type=MESH)

    loads = [
        pltpu.make_async_copy(bf_hbm, bf, load_sem.at[0]),
        pltpu.make_async_copy(src_hbm, src, load_sem.at[1]),
        pltpu.make_async_copy(slot_hbm, slots, load_sem.at[2]),
        pltpu.make_async_copy(pairs_hbm, pairs, load_sem.at[3]),
        pltpu.make_async_copy(count_hbm, count, load_sem.at[4]),
        pltpu.make_async_copy(outb_hbm, outb, load_sem.at[5]),
        pltpu.make_async_copy(near_hbm, near, load_sem.at[6]),
    ]
    per = leaves // in_sem.shape[0]
    in_loads = [
        pltpu.make_async_copy(inb_hbm.at[pl.ds(i * per, per)], inb.at[pl.ds(i * per, per)], in_sem.at[i])
        for i in range(in_sem.shape[0])
    ]
    for c in [loads[1]] + in_loads[:1] + [loads[0]] + in_loads[1:] + loads[2:5]:
        c.start()

    lane = lax.broadcasted_iota(jnp.int32, (1, rank2), 1)
    sign = jnp.where(lane < rank, 1.0, -1.0).astype(F32)

    def real_form(block):
        return jnp.concatenate([block * sign, pltpu.roll(block, rank, 1)], axis=0).T

    def weights(t):
        return jnp.concatenate(split(t), axis=1)

    def times(xs, wide):
        high, low = zip(*[split(x) for x in xs])
        y = dot(jnp.concatenate([jnp.concatenate(high, axis=1), jnp.concatenate(low, axis=1)], axis=0), wide)
        y = y[:, :rank2] + y[:, rank2:]
        return y[:y.shape[0] // 2] + y[y.shape[0] // 2:]

    def prepare_single(i):
        b = GROUPS[i][0]
        for k in range(2):
            w[W_FIRST[i] + k] = weights(real_form(bf[2 * b + k]))

    def prepare_double(i):
        a, b = GROUPS[i]
        d = DOUBLE.index(i)
        for k in range(2):
            wtmp[k] = weights(real_form(bf[2 * b + k]))
        for k in range(2):
            if k == 0:
                lower = [bf[2 * a], bf[2 * a + 1]]
            else:
                bp_copy[d].wait_recv()
                lower = [bp[d, 0], bp[d, 1]]
            t = times([jnp.concatenate([real_form(x) for x in lower], axis=0)], wtmp[k])
            w[W_FIRST[i] + 2 * k] = weights(t[:rank2])
            w[W_FIRST[i] + 2 * k + 1] = weights(t[rank2:])

    def prepare_z_here():
        wtmp[0] = weights(real_form(bf[12]))
        t = times([jnp.concatenate([real_form(bf[10]), real_form(bf[11])], axis=0)], wtmp[0])
        w[W_FAR + 1] = weights(t[:rank2])
        w[W_OWN] = weights(t[:rank2])
        w[W_OWN + 1] = weights(t[rank2:])
        m_out[...] = t[rank2:]
        for k in range(2):
            w[W_LAST + k] = weights(real_form(bf[14 + k]))

    def prepare_z_there():
        m_copy[0].wait_recv()
        w[W_FAR] = weights(m_in[...])
        m_copy[1].wait_recv()
        wtmp[0] = weights(real_form(b_in[...]))
        t = times([jnp.concatenate([real_form(bf[10]), real_form(bf[11])], axis=0)], wtmp[0])
        for k in range(2):
            w[W_NEAR + k] = weights(t[k * rank2:(k + 1) * rank2])

    def chunk(c):
        return pl.ds(START[c] * width, CHUNK_LEAVES[c] * width)

    def copy_to(ref, i, e, c):
        return pltpu.make_async_remote_copy(
            src_ref=ref.at[chunk(c)], dst_ref=recv.at[FIRST[i] + e, chunk(c)],
            send_sem=p_send.at[int(i == Z2 and e == 0)], recv_sem=p_recv.at[i, c],
            device_id=(me ^ MASKS[i][e],), device_id_type=MESH)

    def send(i, c):
        for e in range(len(MASKS[i]))[::-1]:
            copy_to(panel.at[i], i, e, c).start()

    def arrive(i, c):
        skip = int(i == Z2 and c < DIRECT)
        ref = recv.at[pl.ds(FIRST[i] + skip, len(MASKS[i]) - skip), chunk(c)]
        pltpu.make_async_copy(ref, ref, p_recv.at[i, c]).wait()

    bp_copy = [
        pltpu.make_async_remote_copy(
            src_ref=bf.at[pl.ds(2 * GROUPS[i][0], 2)], dst_ref=bp.at[d],
            send_sem=bp_send.at[0], recv_sem=bp_recv.at[d],
            device_id=(me ^ (1 << GROUPS[i][1]),), device_id_type=MESH)
        for d, i in enumerate(DOUBLE)
    ]
    m_copy = [
        pltpu.make_async_remote_copy(
            src_ref=ref, dst_ref=to, send_sem=m_send.at[k], recv_sem=m_recv.at[k],
            device_id=(me ^ m,), device_id_type=MESH)
        for k, (ref, to, m) in enumerate(((m_out, m_in, 32), (bf.at[13], b_in, 64)))
    ]
    halo_copy = [
        pltpu.make_async_remote_copy(
            src_ref=pack.at[pl.ds(h * HALO, HALO)], dst_ref=halo.at[pl.ds(h * HALO, HALO)],
            send_sem=halo_send.at[0], recv_sem=halo_recv.at[h], device_id=(to,), device_id_type=MESH)
        for h, to in ((0, nxt), (1, prv))
    ]

    def tell(k, to):
        pl.semaphore_signal(known.at[k], inc=1, device_id=(to,), device_id_type=MESH)

    loads[1].wait()

    def coeff(j, carry):
        x = jnp.concatenate([src[0, j], src[1, j]], axis=0)
        y = dot_nt(jnp.concatenate(split(x), axis=0), jnp.concatenate(split(inb[j]), axis=0))
        y = y[:16] + y[16:]
        y = y[:, :rank2] + y[:, rank2:]
        panel[0, pl.ds(pl.multiple_of(j * 8, 8), 8)] = y[:8] - sign * pltpu.roll(y[8:], rank, 1)
        return carry

    waited = 0
    for c in range(CHUNKS):
        count_in = -(-START[c + 1] // per)
        for i in range(waited, count_in):
            in_loads[i].wait()
        waited = count_in
        lax.fori_loop(START[c], START[c + 1], coeff, 0, unroll=True)
        if c == 0:
            pl.semaphore_wait(barrier, len(neighbours))
        if c == 0:
            loads[0].wait()
            bp_copy[0].start()
        send(0, c)
        if c == 0:
            bp_copy[1].start()

    tell(2, up)
    tell(2, down)
    prepare_single(0)

    def pack_halo():
        loads[2].wait()
        for h in range(2):
            for i in range(HALO):
                leaf = base + (leaves - HALO + i if h == 0 else i)
                where = jnp.clip(slots[leaf] - base, 0, leaves - 1)
                pack[h * HALO + i] = src[:, where]
            halo_copy[h].start()

    def prepare_out(j, carry):
        high, low = split(outb[j])
        obf[j, pl.ds(0, rank2)] = high
        obf[j, pl.ds(rank2, rank2)] = low
        return carry

    leaf_iota = lax.broadcasted_iota(jnp.int32, (leaves, 1, 1), 0)

    def near_term(k, carry):
        a, t = pairs[0, k], pairs[1, k]
        own = jnp.clip(slots[a] - base, 0, leaves - 1)
        off = jnp.clip(jnp.where(a < base, a - base + HALO, a - base - leaves + HALO), 0, 2 * HALO - 1)
        inside = jnp.logical_and(a >= base, a < base + leaves)
        x = jnp.where(inside, src[:, own], halo[off]).reshape(16, -1)
        high, low = split(x)
        both = jnp.concatenate([high, low], axis=0)
        y = []
        for q in range(2):
            bh, bl = split(near[k, q])
            yh, yl = dot_nt(both, bh), dot_nt(high, bl)
            y.append(yh[:16] + yh[16:] + yl)
        hit = jnp.logical_and(leaf_iota == slots[t] - base, k < count[0])
        nacc[0] += jnp.where(hit, (y[0][:8] - y[1][8:])[None], 0.0)
        nacc[1] += jnp.where(hit, (y[0][8:] + y[1][:8])[None], 0.0)
        return carry

    def background(i):
        if i == 0:
            pl.semaphore_wait(known.at[2], 2)
            tell(3, me ^ 64)
            tell(3, me ^ 192)
        if i == 1:
            loads[5].start()
            prepare_z_here()
            m_copy[0].start()
            m_copy[1].start()
            prepare_double(1)
        if i == 2:
            loads[6].start()
            pack_halo()
            prepare_double(2)
            pl.semaphore_wait(known.at[3], 2)
            prepare_z_there()
        if i == 3:
            loads[5].wait()
            lax.fori_loop(0, leaves, prepare_out, 0)
        if i == 4:
            loads[3].wait()
            loads[4].wait()
            loads[6].wait()
            nacc[...] = jnp.zeros_like(nacc)
            for cp in halo_copy:
                cp.wait_recv()
            lax.fori_loop(0, 8, near_term, 0)

    def far(acc, j, r):
        x = acc[r:r + width]
        high, low = split(jnp.concatenate([x * sign, pltpu.roll(x, rank, 1)], axis=0))
        lhs = jnp.concatenate(
            [jnp.concatenate([high, high], axis=1), jnp.concatenate([low, low], axis=1)], axis=0)
        y = dot(lhs, obf[j])
        y = y[:16] + y[16:]
        out_ref[0, j] = y[:8] + nacc[0, j]
        out_ref[1, j] = y[8:] + nacc[1, j]

    def stacked(first, blocks):
        return w[pl.ds(first, blocks)].reshape(blocks * rank2, 2 * rank2)

    def got(i, e, c):
        return recv[FIRST[i] + e, chunk(c)]

    for i in range(len(GROUPS)):
        background(i)
        blocks = len(MASKS[i]) + 1
        for c in range(CHUNKS):
            arrive(i, c)
            xs = [panel[i, chunk(c)]] + [got(i, e, c) for e in range(blocks - 1)]
            acc = times(xs, stacked(W_FIRST[i], blocks))
            panel[i + 1, chunk(c)] = acc
            send(i + 1, c)
            if i + 1 == Z1 and c >= DIRECT:
                for k in (1, 0):
                    z_panel[k, chunk(c)] = times([acc], w[W_FAR + k])
                    copy_to(z_panel.at[k], Z2, k, c).start()

    background(Z1)
    for c in range(CHUNKS):
        arrive(Z1, c)
        xs = [panel[Z1, chunk(c)], got(Z1, 0, c)]
        if c < DIRECT:
            z_panel[1, chunk(c)] = times(xs, stacked(W_OWN, 2))
            copy_to(z_panel.at[1], Z2, 1, c).start()
        z_panel[2, chunk(c)] = times(xs, stacked(W_NEAR, 2))
        for e in (2, 3):
            copy_to(z_panel.at[2], Z2, e, c).start()
        if c >= DIRECT:
            z_own[chunk(c)] = times(xs, stacked(W_OWN, 2))

    background(Z2)
    for c in range(CHUNKS):
        arrive(Z2, c)
        here, there = z_panel[1, chunk(c)] if c < DIRECT else z_own[chunk(c)], got(Z2, 1, c) + got(Z2, 3, c)
        if c >= DIRECT:
            there = there + got(Z2, 0, c)
        xs = [here + got(Z2, 2, c), there]
        acc = times(xs, stacked(W_LAST, 2))
        for j in range(START[c], START[c + 1]):
            far(acc, j, (j - START[c]) * width)

    for cp in m_copy:
        cp.wait_send()
    skipped = FIRST[Z2]
    for ref, sem in ((recv.at[pl.ds(0, skipped)], p_send.at[0]), (recv.at[pl.ds(skipped + 1, 3)], p_send.at[0]),
                     (bp, bp_send.at[0]), (pack, halo_send.at[0])):
        pltpu.make_async_copy(ref, ref, sem).wait()
    if DIRECT < CHUNKS:
        ref = recv.at[skipped, pl.ds(START[DIRECT] * width, (leaves - START[DIRECT]) * width)]
        pltpu.make_async_copy(ref, ref, p_send.at[1]).wait()


def body(sources, leaf_slot, in_basis, butterfly, out_basis, near_pairs, near_count, near_blocks):
    leaves, s, size = sources.shape[1:]
    rank = in_basis.shape[2]
    levels = butterfly.shape[0]
    slots = near_pairs.shape[0]
    rows = leaves * s
    any_spec = pl.BlockSpec(memory_space=pltpu.HBM)
    dma = pltpu.SemaphoreType.DMA
    return pl.pallas_call(
        kernel,
        out_shape=pltpu.VMEM(sources.shape, F32),
        in_specs=[any_spec] * 8,
        out_specs=pl.BlockSpec(memory_space=pltpu.VMEM),
        scratch_shapes=[
            pltpu.VMEM(sources.shape, F32),
            pltpu.VMEM((leaves, 2 * rank, size), F32),
            pltpu.VMEM((2 * levels, rank, 2 * rank), F32),
            pltpu.VMEM((leaves, 2 * rank, size), F32),
            pltpu.VMEM(near_blocks.shape, F32),
            pltpu.SMEM(leaf_slot.shape, jnp.int32),
            pltpu.SMEM(near_pairs.shape[::-1], jnp.int32),
            pltpu.SMEM(near_count.shape, jnp.int32),
            pltpu.VMEM((len(DOUBLE), 2, rank, 2 * rank), F32),
            pltpu.VMEM((2 * HALO, 2, s, size), F32),
            pltpu.VMEM((2 * HALO, 2, s, size), F32),
            pltpu.VMEM((N_W, 2 * rank, 4 * rank), BF16),
            pltpu.VMEM((2, 2 * rank, 4 * rank), BF16),
            pltpu.VMEM((leaves, 4 * rank, size), BF16),
            pltpu.VMEM(sources.shape, F32),
            pltpu.VMEM((Z1 + 1, rows, 2 * rank), F32),
            pltpu.VMEM((N_RECV, rows, 2 * rank), F32),
            pltpu.VMEM((3, rows, 2 * rank), F32),
            pltpu.VMEM((rows, 2 * rank), F32),
            pltpu.VMEM((2 * rank, 2 * rank), F32),
            pltpu.VMEM((2 * rank, 2 * rank), F32),
            pltpu.VMEM((rank, 2 * rank), F32),
            dma((7,)),
            dma((4,)),
            dma((1,)),
            dma((len(DOUBLE),)),
            dma((2,)),
            dma((2,)),
            dma((1,)),
            dma((2,)),
            dma((2,)),
            dma((len(MASKS), CHUNKS)),
            pltpu.SemaphoreType.REGULAR((4,)),
        ],
        compiler_params=pltpu.CompilerParams(
            collective_id=0, has_side_effects=True, vmem_limit_bytes=60 * 1024 * 1024),
        name="butterfly",
    )(sources, leaf_slot, in_basis.reshape(leaves, 2 * rank, size),
      butterfly.reshape(2 * levels, rank, 2 * rank), out_basis.reshape(leaves, 2 * rank, size),
      near_pairs.T, near_count, near_blocks)


def solution(mesh):
    in_specs = (
        P(None, "leaf", None, None),
        P(),
        P("leaf", None, None, None),
        P(None, "leaf", None, None, None),
        P("leaf", None, None, None),
        P("leaf", None),
        P("leaf"),
        P("leaf", None, None, None),
    )
    out_specs = P(None, "leaf", None, None)
    return jax.shard_map(body, mesh=mesh, in_specs=in_specs, out_specs=out_specs, check_vma=False)
```

```python
import functools

import jax
import jax.numpy as jnp
from jax import lax
from jax.experimental import pallas as pl
from jax.experimental.pallas import tpu as pltpu
from jax.sharding import PartitionSpec as P

MESH = pl.DeviceIdType.MESH
F32, BF16 = jnp.float32, jnp.bfloat16
GROUPS = ((0,), (1, 2), (3, 4))
CHUNK_LEAVES = (4, 4, 4, 4)
CHUNKS = len(CHUNK_LEAVES)
DIRECT = 2
START = tuple(sum(CHUNK_LEAVES[:c]) for c in range(CHUNKS + 1))
HALO = 4


def masks_of(group):
    if len(group) == 1:
        return (1 << group[0],)
    low, high = 1 << group[0], 1 << group[1]
    return (low, high, low | high)


Z1, Z2 = 3, 4
MASKS = tuple(masks_of(g) for g in GROUPS) + ((32,), (160, 128, 64, 192))
FIRST = tuple(sum(len(m) for m in MASKS[:i]) for i in range(len(MASKS)))
N_RECV = sum(len(m) for m in MASKS)
W_FIRST = tuple(sum(len(m) + 1 for m in MASKS[:i]) for i in range(len(GROUPS) + 1))
W_FAR, W_NEAR, W_OWN, W_LAST = (W_FIRST[-1] + 2 * i for i in range(4))
N_W = W_FIRST[-1] + 8
DOUBLE = tuple(i for i, g in enumerate(GROUPS) if len(g) == 2)


def split(x):
    high = x.astype(BF16)
    return high, (x - high.astype(F32)).astype(BF16)


def dot(a, b):
    return jnp.dot(a, b, preferred_element_type=F32)


def dot_nt(a, b):
    return lax.dot_general(a, b, (((1,), (1,)), ((), ())), preferred_element_type=F32)


def far_rows(x, basis):
    rank = x.shape[1] // 2
    sign = jnp.where(lax.broadcasted_iota(jnp.int32, (1, 2 * rank), 1) < rank, 1.0, -1.0).astype(F32)
    high, low = split(jnp.concatenate([x * sign, pltpu.roll(x, rank, 1)], axis=0))
    lhs = jnp.concatenate(
        [jnp.concatenate([high, high], axis=1), jnp.concatenate([low, low], axis=1)], axis=0)
    y = dot(lhs, basis)
    return y[:16] + y[16:]


def store(field, last, obf, nacc, out, tail, sem):
    lead, each = START[-2], CHUNK_LEAVES[-1]
    copies = [pltpu.make_async_copy(field.at[q, pl.ds(0, lead)], out.at[q, pl.ds(0, lead)], sem.at[q]) for q in range(2)]
    for cp in copies:
        cp.start()
    for j in range(each):
        y = far_rows(last[pl.ds(8 * j, 8)], obf[lead + j])
        tail[0, j] = y[:8] + nacc[0, lead + j]
        tail[1, j] = y[8:] + nacc[1, lead + j]
    for q in range(2):
        copies.append(pltpu.make_async_copy(tail.at[q], out.at[q, pl.ds(lead, each)], sem.at[2 + q]))
        copies[-1].start()
    for cp in copies:
        cp.wait()


def kernel(src_hbm, slot_hbm, inb_hbm, bf_hbm, outb_hbm, pairs_hbm, count_hbm, near_hbm, out_ref, last_ref, obf, nacc,
           src, inb, bf, outb, near, slots, pairs, count, bp, pack, halo, w, wtmp, panel, recv,
           z_panel, z_own, m_out, m_in, b_in,
           load_sem, in_sem, bp_send, bp_recv, m_send, m_recv, halo_send, halo_recv, p_send, p_recv, known):
    n = lax.axis_size("leaf")
    me = lax.axis_index("leaf")
    nxt, prv = lax.rem(me + 1, n), lax.rem(me + n - 1, n)
    leaves = src.shape[1]
    base = me * leaves
    width = panel.shape[1] // leaves
    rank2 = panel.shape[2]
    rank = rank2 // 2

    step = MASKS[Z1][0]
    up, down = lax.rem(me + step, n), lax.rem(me + n - step, n)
    barrier = pltpu.get_barrier_semaphore()
    neighbours = [me ^ 1, me ^ 2, me ^ 4, me ^ 6, me ^ 8, me ^ 16, me ^ 24, up, down, nxt, prv]
    for p in neighbours:
        pl.semaphore_signal(barrier, inc=1, device_id=(p,), device_id_type=MESH)

    loads = [
        pltpu.make_async_copy(bf_hbm, bf, load_sem.at[0]),
        pltpu.make_async_copy(src_hbm, src, load_sem.at[1]),
        pltpu.make_async_copy(slot_hbm, slots, load_sem.at[2]),
        pltpu.make_async_copy(pairs_hbm, pairs, load_sem.at[3]),
        pltpu.make_async_copy(count_hbm, count, load_sem.at[4]),
        pltpu.make_async_copy(outb_hbm, outb, load_sem.at[5]),
        pltpu.make_async_copy(near_hbm, near, load_sem.at[6]),
    ]
    per = leaves // in_sem.shape[0]
    in_loads = [
        pltpu.make_async_copy(inb_hbm.at[pl.ds(i * per, per)], inb.at[pl.ds(i * per, per)], in_sem.at[i])
        for i in range(in_sem.shape[0])
    ]
    for c in [loads[1]] + in_loads[:1] + [loads[0]] + in_loads[1:] + loads[2:5]:
        c.start()

    lane = lax.broadcasted_iota(jnp.int32, (1, rank2), 1)
    sign = jnp.where(lane < rank, 1.0, -1.0).astype(F32)

    def real_form(block):
        return jnp.concatenate([block * sign, pltpu.roll(block, rank, 1)], axis=0).T

    def weights(t):
        return jnp.concatenate(split(t), axis=1)

    def times(xs, wide):
        high, low = zip(*[split(x) for x in xs])
        y = dot(jnp.concatenate([jnp.concatenate(high, axis=1), jnp.concatenate(low, axis=1)], axis=0), wide)
        y = y[:, :rank2] + y[:, rank2:]
        return y[:y.shape[0] // 2] + y[y.shape[0] // 2:]

    def prepare_single(i):
        b = GROUPS[i][0]
        for k in range(2):
            w[W_FIRST[i] + k] = weights(real_form(bf[2 * b + k]))

    def prepare_double(i):
        a, b = GROUPS[i]
        d = DOUBLE.index(i)
        for k in range(2):
            wtmp[k] = weights(real_form(bf[2 * b + k]))
        for k in range(2):
            if k == 0:
                lower = [bf[2 * a], bf[2 * a + 1]]
            else:
                bp_copy[d].wait_recv()
                lower = [bp[d, 0], bp[d, 1]]
            t = times([jnp.concatenate([real_form(x) for x in lower], axis=0)], wtmp[k])
            w[W_FIRST[i] + 2 * k] = weights(t[:rank2])
            w[W_FIRST[i] + 2 * k + 1] = weights(t[rank2:])

    def prepare_z_here():
        wtmp[0] = weights(real_form(bf[12]))
        t = times([jnp.concatenate([real_form(bf[10]), real_form(bf[11])], axis=0)], wtmp[0])
        w[W_FAR + 1] = weights(t[:rank2])
        w[W_OWN] = weights(t[:rank2])
        w[W_OWN + 1] = weights(t[rank2:])
        m_out[...] = t[rank2:]
        for k in range(2):
            w[W_LAST + k] = weights(real_form(bf[14 + k]))

    def prepare_z_there():
        m_copy[0].wait_recv()
        w[W_FAR] = weights(m_in[...])
        m_copy[1].wait_recv()
        wtmp[0] = weights(real_form(b_in[...]))
        t = times([jnp.concatenate([real_form(bf[10]), real_form(bf[11])], axis=0)], wtmp[0])
        for k in range(2):
            w[W_NEAR + k] = weights(t[k * rank2:(k + 1) * rank2])

    def chunk(c):
        return pl.ds(START[c] * width, CHUNK_LEAVES[c] * width)

    def copy_to(ref, i, e, c):
        return pltpu.make_async_remote_copy(
            src_ref=ref.at[chunk(c)], dst_ref=recv.at[FIRST[i] + e, chunk(c)],
            send_sem=p_send.at[int(i == Z2 and e == 0)], recv_sem=p_recv.at[i, c],
            device_id=(me ^ MASKS[i][e],), device_id_type=MESH)

    def send(i, c):
        for e in range(len(MASKS[i]))[::-1]:
            copy_to(panel.at[i], i, e, c).start()

    def arrive(i, c):
        skip = int(i == Z2 and c < DIRECT)
        ref = recv.at[pl.ds(FIRST[i] + skip, len(MASKS[i]) - skip), chunk(c)]
        pltpu.make_async_copy(ref, ref, p_recv.at[i, c]).wait()

    bp_copy = [
        pltpu.make_async_remote_copy(
            src_ref=bf.at[pl.ds(2 * GROUPS[i][0], 2)], dst_ref=bp.at[d],
            send_sem=bp_send.at[0], recv_sem=bp_recv.at[d],
            device_id=(me ^ (1 << GROUPS[i][1]),), device_id_type=MESH)
        for d, i in enumerate(DOUBLE)
    ]
    m_copy = [
        pltpu.make_async_remote_copy(
            src_ref=ref, dst_ref=to, send_sem=m_send.at[k], recv_sem=m_recv.at[k],
            device_id=(me ^ m,), device_id_type=MESH)
        for k, (ref, to, m) in enumerate(((m_out, m_in, 32), (bf.at[13], b_in, 64)))
    ]
    halo_copy = [
        pltpu.make_async_remote_copy(
            src_ref=pack.at[pl.ds(h * HALO, HALO)], dst_ref=halo.at[pl.ds(h * HALO, HALO)],
            send_sem=halo_send.at[0], recv_sem=halo_recv.at[h], device_id=(to,), device_id_type=MESH)
        for h, to in ((0, nxt), (1, prv))
    ]

    def tell(k, to):
        pl.semaphore_signal(known.at[k], inc=1, device_id=(to,), device_id_type=MESH)

    loads[1].wait()

    def coeff(j, carry):
        x = jnp.concatenate([src[0, j], src[1, j]], axis=0)
        y = dot_nt(jnp.concatenate(split(x), axis=0), jnp.concatenate(split(inb[j]), axis=0))
        y = y[:16] + y[16:]
        y = y[:, :rank2] + y[:, rank2:]
        panel[0, pl.ds(pl.multiple_of(j * 8, 8), 8)] = y[:8] - sign * pltpu.roll(y[8:], rank, 1)
        return carry

    waited = 0
    for c in range(CHUNKS):
        count_in = -(-START[c + 1] // per)
        for i in range(waited, count_in):
            in_loads[i].wait()
        waited = count_in
        lax.fori_loop(START[c], START[c + 1], coeff, 0, unroll=True)
        if c == 0:
            pl.semaphore_wait(barrier, len(neighbours))
        if c == 0:
            loads[0].wait()
            bp_copy[0].start()
        send(0, c)
        if c == 0:
            bp_copy[1].start()

    tell(2, up)
    tell(2, down)
    prepare_single(0)

    def pack_halo():
        loads[2].wait()
        for h in range(2):
            for i in range(HALO):
                leaf = base + (leaves - HALO + i if h == 0 else i)
                where = jnp.clip(slots[leaf] - base, 0, leaves - 1)
                pack[h * HALO + i] = src[:, where]
            halo_copy[h].start()

    def prepare_out(j, carry):
        high, low = split(outb[j])
        obf[j, pl.ds(0, rank2)] = high
        obf[j, pl.ds(rank2, rank2)] = low
        return carry

    leaf_iota = lax.broadcasted_iota(jnp.int32, (leaves, 1, 1), 0)

    def near_term(k, carry):
        a, t = pairs[0, k], pairs[1, k]
        own = jnp.clip(slots[a] - base, 0, leaves - 1)
        off = jnp.clip(jnp.where(a < base, a - base + HALO, a - base - leaves + HALO), 0, 2 * HALO - 1)
        inside = jnp.logical_and(a >= base, a < base + leaves)
        x = jnp.where(inside, src[:, own], halo[off]).reshape(16, -1)
        high, low = split(x)
        both = jnp.concatenate([high, low], axis=0)
        y = []
        for q in range(2):
            bh, bl = split(near[k, q])
            yh, yl = dot_nt(both, bh), dot_nt(high, bl)
            y.append(yh[:16] + yh[16:] + yl)
        hit = jnp.logical_and(leaf_iota == slots[t] - base, k < count[0])
        nacc[0] += jnp.where(hit, (y[0][:8] - y[1][8:])[None], 0.0)
        nacc[1] += jnp.where(hit, (y[0][8:] + y[1][:8])[None], 0.0)
        return carry

    def background(i):
        if i == 0:
            pl.semaphore_wait(known.at[2], 2)
            tell(3, me ^ 64)
            tell(3, me ^ 192)
        if i == 1:
            loads[5].start()
            prepare_z_here()
            m_copy[0].start()
            m_copy[1].start()
            prepare_double(1)
        if i == 2:
            loads[6].start()
            pack_halo()
            prepare_double(2)
            pl.semaphore_wait(known.at[3], 2)
            prepare_z_there()
        if i == 3:
            loads[5].wait()
            lax.fori_loop(0, leaves, prepare_out, 0)
        if i == 4:
            loads[3].wait()
            loads[4].wait()
            loads[6].wait()
            nacc[...] = jnp.zeros_like(nacc)
            for cp in halo_copy:
                cp.wait_recv()
            lax.fori_loop(0, 8, near_term, 0)

    def stacked(first, blocks):
        return w[pl.ds(first, blocks)].reshape(blocks * rank2, 2 * rank2)

    def got(i, e, c):
        return recv[FIRST[i] + e, chunk(c)]

    for i in range(len(GROUPS)):
        background(i)
        blocks = len(MASKS[i]) + 1
        for c in range(CHUNKS):
            arrive(i, c)
            xs = [panel[i, chunk(c)]] + [got(i, e, c) for e in range(blocks - 1)]
            acc = times(xs, stacked(W_FIRST[i], blocks))
            panel[i + 1, chunk(c)] = acc
            send(i + 1, c)
            if i + 1 == Z1 and c >= DIRECT:
                for k in (1, 0):
                    z_panel[k, chunk(c)] = times([acc], w[W_FAR + k])
                    copy_to(z_panel.at[k], Z2, k, c).start()

    background(Z1)
    for c in range(CHUNKS):
        arrive(Z1, c)
        xs = [panel[Z1, chunk(c)], got(Z1, 0, c)]
        if c < DIRECT:
            z_panel[1, chunk(c)] = times(xs, stacked(W_OWN, 2))
            copy_to(z_panel.at[1], Z2, 1, c).start()
        z_panel[2, chunk(c)] = times(xs, stacked(W_NEAR, 2))
        for e in (2, 3):
            copy_to(z_panel.at[2], Z2, e, c).start()
        if c >= DIRECT:
            z_own[chunk(c)] = times(xs, stacked(W_OWN, 2))

    background(Z2)
    for c in range(CHUNKS):
        arrive(Z2, c)
        here, there = z_panel[1, chunk(c)] if c < DIRECT else z_own[chunk(c)], got(Z2, 1, c) + got(Z2, 3, c)
        if c >= DIRECT:
            there = there + got(Z2, 0, c)
        xs = [here + got(Z2, 2, c), there]
        acc = times(xs, stacked(W_LAST, 2))
        if c == CHUNKS - 1:
            last_ref[...] = acc
            continue
        for j in range(START[c], START[c + 1]):
            r = (j - START[c]) * width
            y = far_rows(acc[r:r + width], obf[j])
            out_ref[0, j] = y[:8] + nacc[0, j]
            out_ref[1, j] = y[8:] + nacc[1, j]

    for cp in m_copy:
        cp.wait_send()
    skipped = FIRST[Z2]
    for ref, sem in ((recv.at[pl.ds(0, skipped)], p_send.at[0]), (recv.at[pl.ds(skipped + 1, 3)], p_send.at[0]),
                     (bp, bp_send.at[0]), (pack, halo_send.at[0])):
        pltpu.make_async_copy(ref, ref, sem).wait()
    if DIRECT < CHUNKS:
        ref = recv.at[skipped, pl.ds(START[DIRECT] * width, (leaves - START[DIRECT]) * width)]
        pltpu.make_async_copy(ref, ref, p_send.at[1]).wait()


def body(sources, leaf_slot, in_basis, butterfly, out_basis, near_pairs, near_count, near_blocks):
    leaves, s, size = sources.shape[1:]
    rank = in_basis.shape[2]
    levels = butterfly.shape[0]
    slots = near_pairs.shape[0]
    rows = leaves * s
    any_spec = pl.BlockSpec(memory_space=pltpu.HBM)
    dma = pltpu.SemaphoreType.DMA
    vmem = pl.BlockSpec(memory_space=pltpu.VMEM)
    parts = pl.pallas_call(
        kernel,
        out_shape=(
            pltpu.VMEM(sources.shape, F32),
            pltpu.VMEM((CHUNK_LEAVES[-1] * s, 2 * rank), F32),
            pltpu.VMEM((leaves, 4 * rank, size), BF16),
            pltpu.VMEM(sources.shape, F32),
        ),
        in_specs=[any_spec] * 8,
        out_specs=(vmem,) * 4,
        scratch_shapes=[
            pltpu.VMEM(sources.shape, F32),
            pltpu.VMEM((leaves, 2 * rank, size), F32),
            pltpu.VMEM((2 * levels, rank, 2 * rank), F32),
            pltpu.VMEM((leaves, 2 * rank, size), F32),
            pltpu.VMEM(near_blocks.shape, F32),
            pltpu.SMEM(leaf_slot.shape, jnp.int32),
            pltpu.SMEM(near_pairs.shape[::-1], jnp.int32),
            pltpu.SMEM(near_count.shape, jnp.int32),
            pltpu.VMEM((len(DOUBLE), 2, rank, 2 * rank), F32),
            pltpu.VMEM((2 * HALO, 2, s, size), F32),
            pltpu.VMEM((2 * HALO, 2, s, size), F32),
            pltpu.VMEM((N_W, 2 * rank, 4 * rank), BF16),
            pltpu.VMEM((2, 2 * rank, 4 * rank), BF16),
            pltpu.VMEM((Z1 + 1, rows, 2 * rank), F32),
            pltpu.VMEM((N_RECV, rows, 2 * rank), F32),
            pltpu.VMEM((3, rows, 2 * rank), F32),
            pltpu.VMEM((rows, 2 * rank), F32),
            pltpu.VMEM((2 * rank, 2 * rank), F32),
            pltpu.VMEM((2 * rank, 2 * rank), F32),
            pltpu.VMEM((rank, 2 * rank), F32),
            dma((7,)),
            dma((4,)),
            dma((1,)),
            dma((len(DOUBLE),)),
            dma((2,)),
            dma((2,)),
            dma((1,)),
            dma((2,)),
            dma((2,)),
            dma((len(MASKS), CHUNKS)),
            pltpu.SemaphoreType.REGULAR((4,)),
        ],
        compiler_params=pltpu.CompilerParams(
            collective_id=0, has_side_effects=True, vmem_limit_bytes=54 * 1024 * 1024),
        name="butterfly",
    )(sources, leaf_slot, in_basis.reshape(leaves, 2 * rank, size),
      butterfly.reshape(2 * levels, rank, 2 * rank), out_basis.reshape(leaves, 2 * rank, size),
      near_pairs.T, near_count, near_blocks)
    return pl.pallas_call(
        store,
        out_shape=jax.ShapeDtypeStruct(sources.shape, F32),
        in_specs=[vmem] * 4,
        out_specs=any_spec,
        scratch_shapes=[pltpu.VMEM((2, CHUNK_LEAVES[-1], s, size), F32), dma((4,))],
        name="store",
    )(*[pltpu.with_memory_space_constraint(x, pltpu.VMEM) for x in parts])


def solution(mesh):
    in_specs = (
        P(None, "leaf", None, None),
        P(),
        P("leaf", None, None, None),
        P(None, "leaf", None, None, None),
        P("leaf", None, None, None),
        P("leaf", None),
        P("leaf"),
        P("leaf", None, None, None),
    )
    out_specs = P(None, "leaf", None, None)
    return jax.shard_map(body, mesh=mesh, in_specs=in_specs, out_specs=out_specs, check_vma=False)
```

```python
import functools

import jax
import jax.numpy as jnp
from jax import lax
from jax.experimental import pallas as pl
from jax.experimental.pallas import tpu as pltpu
from jax.sharding import PartitionSpec as P

MESH = pl.DeviceIdType.MESH
F32, BF16 = jnp.float32, jnp.bfloat16
GROUPS = ((0,), (1, 2), (3, 4))
CHUNK_LEAVES = (4, 4, 4, 4)
CHUNKS = len(CHUNK_LEAVES)
DIRECT = 2
START = tuple(sum(CHUNK_LEAVES[:c]) for c in range(CHUNKS + 1))
HALO = 4


def masks_of(group):
    if len(group) == 1:
        return (1 << group[0],)
    low, high = 1 << group[0], 1 << group[1]
    return (low, high, low | high)


Z1, Z2 = 3, 4
MASKS = tuple(masks_of(g) for g in GROUPS) + ((32,), (160, 128, 64, 192))
FIRST = tuple(sum(len(m) for m in MASKS[:i]) for i in range(len(MASKS)))
N_RECV = sum(len(m) for m in MASKS)
W_FIRST = tuple(sum(len(m) + 1 for m in MASKS[:i]) for i in range(len(GROUPS) + 1))
W_FAR, W_NEAR, W_OWN, W_LAST = (W_FIRST[-1] + 2 * i for i in range(4))
N_W = W_FIRST[-1] + 8
DOUBLE = tuple(i for i, g in enumerate(GROUPS) if len(g) == 2)


def split(x):
    high = x.astype(BF16)
    return high, (x - high.astype(F32)).astype(BF16)


def dot(a, b):
    return jnp.dot(a, b, preferred_element_type=F32)


def dot_nt(a, b):
    return lax.dot_general(a, b, (((1,), (1,)), ((), ())), preferred_element_type=F32)


def far_rows(x, basis):
    rank = x.shape[1] // 2
    sign = jnp.where(lax.broadcasted_iota(jnp.int32, (1, 2 * rank), 1) < rank, 1.0, -1.0).astype(F32)
    high, low = split(jnp.concatenate([x * sign, pltpu.roll(x, rank, 1)], axis=0))
    lhs = jnp.concatenate(
        [jnp.concatenate([high, high], axis=1), jnp.concatenate([low, low], axis=1)], axis=0)
    y = dot(lhs, basis)
    return y[:16] + y[16:]


def store(field, last, obf, nacc, out, tail, sem):
    lead, each = START[-2], CHUNK_LEAVES[-1]
    copies = [pltpu.make_async_copy(field.at[q, pl.ds(0, lead)], out.at[q, pl.ds(0, lead)], sem.at[q]) for q in range(2)]
    for cp in copies:
        cp.start()
    for j in range(each):
        y = far_rows(last[pl.ds(8 * j, 8)], obf[lead + j])
        tail[0, j] = y[:8] + nacc[0, lead + j]
        tail[1, j] = y[8:] + nacc[1, lead + j]
    for q in range(2):
        copies.append(pltpu.make_async_copy(tail.at[q], out.at[q, pl.ds(lead, each)], sem.at[2 + q]))
        copies[-1].start()
    for cp in copies:
        cp.wait()


def kernel(src_hbm, slot_hbm, inb_hbm, bf_hbm, outb_hbm, pairs_hbm, count_hbm, near_hbm, out_ref, last_ref, obf, nacc,
           src, inb, bf, outb, near, slots, pairs, count, bp, pack, halo, w, wtmp, panel, recv,
           z_panel, z_own, m_out, m_in, b_in,
           load_sem, in_sem, bp_send, bp_recv, m_send, m_recv, halo_send, halo_recv, p_send, p_recv, known):
    n = lax.axis_size("leaf")
    me = lax.axis_index("leaf")
    nxt, prv = lax.rem(me + 1, n), lax.rem(me + n - 1, n)
    leaves = src.shape[1]
    base = me * leaves
    width = panel.shape[1] // leaves
    rank2 = panel.shape[2]
    rank = rank2 // 2

    step = MASKS[Z1][0]
    up, down = lax.rem(me + step, n), lax.rem(me + n - step, n)
    barrier = pltpu.get_barrier_semaphore()
    neighbours = [me ^ 1, me ^ 2, me ^ 4, me ^ 6, me ^ 8, me ^ 16, me ^ 24, up, down, nxt, prv]
    for p in neighbours:
        pl.semaphore_signal(barrier, inc=1, device_id=(p,), device_id_type=MESH)

    loads = [
        pltpu.make_async_copy(bf_hbm, bf, load_sem.at[0]),
        pltpu.make_async_copy(src_hbm, src, load_sem.at[1]),
        pltpu.make_async_copy(slot_hbm, slots, load_sem.at[2]),
        pltpu.make_async_copy(pairs_hbm, pairs, load_sem.at[3]),
        pltpu.make_async_copy(count_hbm, count, load_sem.at[4]),
        pltpu.make_async_copy(outb_hbm, outb, load_sem.at[5]),
        pltpu.make_async_copy(near_hbm, near, load_sem.at[6]),
    ]
    per = leaves // in_sem.shape[0]
    in_loads = [
        pltpu.make_async_copy(inb_hbm.at[pl.ds(i * per, per)], inb.at[pl.ds(i * per, per)], in_sem.at[i])
        for i in range(in_sem.shape[0])
    ]
    for c in [loads[1]] + in_loads[:1] + [loads[0]] + in_loads[1:] + loads[2:5]:
        c.start()

    lane = lax.broadcasted_iota(jnp.int32, (1, rank2), 1)
    sign = jnp.where(lane < rank, 1.0, -1.0).astype(F32)

    def real_form(block):
        return jnp.concatenate([block * sign, pltpu.roll(block, rank, 1)], axis=0).T

    def weights(t):
        return jnp.concatenate(split(t), axis=1)

    def times(xs, wide):
        high, low = zip(*[split(x) for x in xs])
        y = dot(jnp.concatenate([jnp.concatenate(high, axis=1), jnp.concatenate(low, axis=1)], axis=0), wide)
        y = y[:, :rank2] + y[:, rank2:]
        return y[:y.shape[0] // 2] + y[y.shape[0] // 2:]

    def prepare_single(i):
        b = GROUPS[i][0]
        for k in range(2):
            w[W_FIRST[i] + k] = weights(real_form(bf[2 * b + k]))

    def prepare_double(i):
        a, b = GROUPS[i]
        d = DOUBLE.index(i)
        for k in range(2):
            wtmp[k] = weights(real_form(bf[2 * b + k]))
        for k in range(2):
            if k == 0:
                lower = [bf[2 * a], bf[2 * a + 1]]
            else:
                bp_copy[d].wait_recv()
                lower = [bp[d, 0], bp[d, 1]]
            t = times([jnp.concatenate([real_form(x) for x in lower], axis=0)], wtmp[k])
            w[W_FIRST[i] + 2 * k] = weights(t[:rank2])
            w[W_FIRST[i] + 2 * k + 1] = weights(t[rank2:])

    def prepare_z_here():
        wtmp[0] = weights(real_form(bf[12]))
        t = times([jnp.concatenate([real_form(bf[10]), real_form(bf[11])], axis=0)], wtmp[0])
        w[W_FAR + 1] = weights(t[:rank2])
        w[W_OWN] = weights(t[:rank2])
        w[W_OWN + 1] = weights(t[rank2:])
        m_out[...] = t[rank2:]
        for k in range(2):
            w[W_LAST + k] = weights(real_form(bf[14 + k]))

    def prepare_z_there():
        m_copy[0].wait_recv()
        w[W_FAR] = weights(m_in[...])
        m_copy[1].wait_recv()
        wtmp[0] = weights(real_form(b_in[...]))
        t = times([jnp.concatenate([real_form(bf[10]), real_form(bf[11])], axis=0)], wtmp[0])
        for k in range(2):
            w[W_NEAR + k] = weights(t[k * rank2:(k + 1) * rank2])

    def chunk(c):
        return pl.ds(START[c] * width, CHUNK_LEAVES[c] * width)

    def copy_to(ref, i, e, c):
        return pltpu.make_async_remote_copy(
            src_ref=ref.at[chunk(c)], dst_ref=recv.at[FIRST[i] + e, chunk(c)],
            send_sem=p_send.at[int(i == Z2 and e == 0)], recv_sem=p_recv.at[i, c],
            device_id=(me ^ MASKS[i][e],), device_id_type=MESH)

    def send(i, c):
        for e in range(len(MASKS[i]))[::-1]:
            copy_to(panel.at[i], i, e, c).start()

    def arrive(i, c):
        skip = int(i == Z2 and c < DIRECT)
        ref = recv.at[pl.ds(FIRST[i] + skip, len(MASKS[i]) - skip), chunk(c)]
        pltpu.make_async_copy(ref, ref, p_recv.at[i, c]).wait()

    bp_copy = [
        pltpu.make_async_remote_copy(
            src_ref=bf.at[pl.ds(2 * GROUPS[i][0], 2)], dst_ref=bp.at[d],
            send_sem=bp_send.at[0], recv_sem=bp_recv.at[d],
            device_id=(me ^ (1 << GROUPS[i][1]),), device_id_type=MESH)
        for d, i in enumerate(DOUBLE)
    ]
    m_copy = [
        pltpu.make_async_remote_copy(
            src_ref=ref, dst_ref=to, send_sem=m_send.at[k], recv_sem=m_recv.at[k],
            device_id=(me ^ m,), device_id_type=MESH)
        for k, (ref, to, m) in enumerate(((m_out, m_in, 32), (bf.at[13], b_in, 64)))
    ]
    halo_copy = [
        pltpu.make_async_remote_copy(
            src_ref=pack.at[pl.ds(h * HALO, HALO)], dst_ref=halo.at[pl.ds(h * HALO, HALO)],
            send_sem=halo_send.at[0], recv_sem=halo_recv.at[h], device_id=(to,), device_id_type=MESH)
        for h, to in ((0, nxt), (1, prv))
    ]

    def tell(k, to):
        pl.semaphore_signal(known.at[k], inc=1, device_id=(to,), device_id_type=MESH)

    loads[1].wait()

    def coeff(j, carry):
        x = jnp.concatenate([src[0, j], src[1, j]], axis=0)
        y = dot_nt(jnp.concatenate(split(x), axis=0), jnp.concatenate(split(inb[j]), axis=0))
        y = y[:16] + y[16:]
        y = y[:, :rank2] + y[:, rank2:]
        panel[0, pl.ds(pl.multiple_of(j * 8, 8), 8)] = y[:8] - sign * pltpu.roll(y[8:], rank, 1)
        return carry

    waited = 0
    for c in range(CHUNKS):
        count_in = -(-START[c + 1] // per)
        for i in range(waited, count_in):
            in_loads[i].wait()
        waited = count_in
        lax.fori_loop(START[c], START[c + 1], coeff, 0, unroll=True)
        if c == 0:
            pl.semaphore_wait(barrier, len(neighbours))
        if c == 0:
            loads[0].wait()
            bp_copy[0].start()
        send(0, c)
        if c == 0:
            bp_copy[1].start()

    tell(2, up)
    tell(2, down)
    prepare_single(0)

    def pack_halo():
        loads[2].wait()
        for h in range(2):
            for i in range(HALO):
                leaf = base + (leaves - HALO + i if h == 0 else i)
                where = jnp.clip(slots[leaf] - base, 0, leaves - 1)
                pack[h * HALO + i] = src[:, where]
            halo_copy[h].start()

    def prepare_out(j, carry):
        high, low = split(outb[j])
        obf[j, pl.ds(0, rank2)] = high
        obf[j, pl.ds(rank2, rank2)] = low
        return carry

    leaf_iota = lax.broadcasted_iota(jnp.int32, (leaves, 1, 1), 0)

    def near_term(k, carry):
        a, t = pairs[0, k], pairs[1, k]
        own = jnp.clip(slots[a] - base, 0, leaves - 1)
        off = jnp.clip(jnp.where(a < base, a - base + HALO, a - base - leaves + HALO), 0, 2 * HALO - 1)
        inside = jnp.logical_and(a >= base, a < base + leaves)
        x = jnp.where(inside, src[:, own], halo[off]).reshape(16, -1)
        high, low = split(x)
        both = jnp.concatenate([high, low], axis=0)
        y = []
        for q in range(2):
            bh, bl = split(near[k, q])
            yh, yl = dot_nt(both, bh), dot_nt(high, bl)
            y.append(yh[:16] + yh[16:] + yl)
        hit = jnp.logical_and(leaf_iota == slots[t] - base, k < count[0])
        nacc[0] += jnp.where(hit, (y[0][:8] - y[1][8:])[None], 0.0)
        nacc[1] += jnp.where(hit, (y[0][8:] + y[1][:8])[None], 0.0)
        return carry

    def background(i):
        if i == 0:
            pl.semaphore_wait(known.at[2], 2)
            tell(3, me ^ 64)
            tell(3, me ^ 192)
        if i == 1:
            loads[5].start()
            prepare_z_here()
            m_copy[0].start()
            m_copy[1].start()
            prepare_double(1)
        if i == 2:
            loads[6].start()
            pack_halo()
            prepare_double(2)
            pl.semaphore_wait(known.at[3], 2)
            prepare_z_there()
        if i == 3:
            loads[5].wait()
            lax.fori_loop(0, leaves, prepare_out, 0)
        if i == 4:
            loads[3].wait()
            loads[4].wait()
            loads[6].wait()
            nacc[...] = jnp.zeros_like(nacc)
            for cp in halo_copy:
                cp.wait_recv()
            lax.fori_loop(0, 8, near_term, 0)

    def stacked(first, blocks):
        return w[pl.ds(first, blocks)].reshape(blocks * rank2, 2 * rank2)

    def got(i, e, c):
        return recv[FIRST[i] + e, chunk(c)]

    for i in range(len(GROUPS)):
        background(i)
        blocks = len(MASKS[i]) + 1
        for c in range(CHUNKS):
            arrive(i, c)
            xs = [panel[i, chunk(c)]] + [got(i, e, c) for e in range(blocks - 1)]
            acc = times(xs, stacked(W_FIRST[i], blocks))
            panel[i + 1, chunk(c)] = acc
            send(i + 1, c)
            if i + 1 == Z1 and c >= DIRECT:
                for k in (1, 0):
                    z_panel[k, chunk(c)] = times([acc], w[W_FAR + k])
                for k in (1, 0):
                    copy_to(z_panel.at[k], Z2, k, c).start()

    background(Z1)
    for c in range(CHUNKS):
        arrive(Z1, c)
        xs = [panel[Z1, chunk(c)], got(Z1, 0, c)]
        if c < DIRECT:
            z_panel[1, chunk(c)] = times(xs, stacked(W_OWN, 2))
            copy_to(z_panel.at[1], Z2, 1, c).start()
        z_panel[2, chunk(c)] = times(xs, stacked(W_NEAR, 2))
        for e in (2, 3):
            copy_to(z_panel.at[2], Z2, e, c).start()
        if c >= DIRECT:
            z_own[chunk(c)] = times(xs, stacked(W_OWN, 2))

    background(Z2)
    for c in range(CHUNKS):
        arrive(Z2, c)
        here, there = z_panel[1, chunk(c)] if c < DIRECT else z_own[chunk(c)], got(Z2, 1, c) + got(Z2, 3, c)
        if c >= DIRECT:
            there = there + got(Z2, 0, c)
        xs = [here + got(Z2, 2, c), there]
        acc = times(xs, stacked(W_LAST, 2))
        if c == CHUNKS - 1:
            last_ref[...] = acc
            continue
        for j in range(START[c], START[c + 1]):
            r = (j - START[c]) * width
            y = far_rows(acc[r:r + width], obf[j])
            out_ref[0, j] = y[:8] + nacc[0, j]
            out_ref[1, j] = y[8:] + nacc[1, j]

    for cp in m_copy:
        cp.wait_send()
    skipped = FIRST[Z2]
    for ref, sem in ((recv.at[pl.ds(0, skipped)], p_send.at[0]), (recv.at[pl.ds(skipped + 1, 3)], p_send.at[0]),
                     (bp, bp_send.at[0]), (pack, halo_send.at[0])):
        pltpu.make_async_copy(ref, ref, sem).wait()
    if DIRECT < CHUNKS:
        ref = recv.at[skipped, pl.ds(START[DIRECT] * width, (leaves - START[DIRECT]) * width)]
        pltpu.make_async_copy(ref, ref, p_send.at[1]).wait()


def body(sources, leaf_slot, in_basis, butterfly, out_basis, near_pairs, near_count, near_blocks):
    leaves, s, size = sources.shape[1:]
    rank = in_basis.shape[2]
    levels = butterfly.shape[0]
    slots = near_pairs.shape[0]
    rows = leaves * s
    any_spec = pl.BlockSpec(memory_space=pltpu.HBM)
    dma = pltpu.SemaphoreType.DMA
    vmem = pl.BlockSpec(memory_space=pltpu.VMEM)
    parts = pl.pallas_call(
        kernel,
        out_shape=(
            pltpu.VMEM(sources.shape, F32),
            pltpu.VMEM((CHUNK_LEAVES[-1] * s, 2 * rank), F32),
            pltpu.VMEM((leaves, 4 * rank, size), BF16),
            pltpu.VMEM(sources.shape, F32),
        ),
        in_specs=[any_spec] * 8,
        out_specs=(vmem,) * 4,
        scratch_shapes=[
            pltpu.VMEM(sources.shape, F32),
            pltpu.VMEM((leaves, 2 * rank, size), F32),
            pltpu.VMEM((2 * levels, rank, 2 * rank), F32),
            pltpu.VMEM((leaves, 2 * rank, size), F32),
            pltpu.VMEM(near_blocks.shape, F32),
            pltpu.SMEM(leaf_slot.shape, jnp.int32),
            pltpu.SMEM(near_pairs.shape[::-1], jnp.int32),
            pltpu.SMEM(near_count.shape, jnp.int32),
            pltpu.VMEM((len(DOUBLE), 2, rank, 2 * rank), F32),
            pltpu.VMEM((2 * HALO, 2, s, size), F32),
            pltpu.VMEM((2 * HALO, 2, s, size), F32),
            pltpu.VMEM((N_W, 2 * rank, 4 * rank), BF16),
            pltpu.VMEM((2, 2 * rank, 4 * rank), BF16),
            pltpu.VMEM((Z1 + 1, rows, 2 * rank), F32),
            pltpu.VMEM((N_RECV, rows, 2 * rank), F32),
            pltpu.VMEM((3, rows, 2 * rank), F32),
            pltpu.VMEM((rows, 2 * rank), F32),
            pltpu.VMEM((2 * rank, 2 * rank), F32),
            pltpu.VMEM((2 * rank, 2 * rank), F32),
            pltpu.VMEM((rank, 2 * rank), F32),
            dma((7,)),
            dma((4,)),
            dma((1,)),
            dma((len(DOUBLE),)),
            dma((2,)),
            dma((2,)),
            dma((1,)),
            dma((2,)),
            dma((2,)),
            dma((len(MASKS), CHUNKS)),
            pltpu.SemaphoreType.REGULAR((4,)),
        ],
        compiler_params=pltpu.CompilerParams(
            collective_id=0, has_side_effects=True, vmem_limit_bytes=54 * 1024 * 1024),
        name="butterfly",
    )(sources, leaf_slot, in_basis.reshape(leaves, 2 * rank, size),
      butterfly.reshape(2 * levels, rank, 2 * rank), out_basis.reshape(leaves, 2 * rank, size),
      near_pairs.T, near_count, near_blocks)
    return pl.pallas_call(
        store,
        out_shape=jax.ShapeDtypeStruct(sources.shape, F32),
        in_specs=[vmem] * 4,
        out_specs=any_spec,
        scratch_shapes=[pltpu.VMEM((2, CHUNK_LEAVES[-1], s, size), F32), dma((4,))],
        name="store",
    )(*[pltpu.with_memory_space_constraint(x, pltpu.VMEM) for x in parts])


def solution(mesh):
    in_specs = (
        P(None, "leaf", None, None),
        P(),
        P("leaf", None, None, None),
        P(None, "leaf", None, None, None),
        P("leaf", None, None, None),
        P("leaf", None),
        P("leaf"),
        P("leaf", None, None, None),
    )
    out_specs = P(None, "leaf", None, None)
    return jax.shard_map(body, mesh=mesh, in_specs=in_specs, out_specs=out_specs, check_vma=False)
```
